1024 devices in a mesh: gx: 16 (over y, x_lo), gy: 4 (over x_hi, core), gz: 16 (over z).
Axes of the slice: x: 4 (x_hi: 2, x_lo: 2; x = x_hi * 2 + x_lo), y: 8, z: 16, core: 2. Of those that a mesh axis runs over, the one named last changes fastest.
Arguments:
- counts: int32 [64, 32, 2048], P('gx', 'gy', 'gz'), may hold values from 0 to 4, as said below
- offsets: float32 [3, 4, 64, 32, 2048], P(None, None, 'gx', 'gy', 'gz'), may hold values from 0 to 1
- volume: float32 [4, 64, 32, 2048], P(None, 'gx', 'gy', 'gz'), may hold values from 0.02 to 0.25
- beta: float32 [4, 64, 32, 2048], P(None, 'gx', 'gy', 'gz'), may hold values from 0.3 to 3
- particle_velocity: float32 [3, 4, 64, 32, 2048], P(None, None, 'gx', 'gy', 'gz'), may hold values from -6 to 6
- gas_velocity: float32 [3, 64, 32, 2048], P(None, 'gx', 'gy', 'gz'), may hold values from -6 to 6
Outputs:
- filtered: float32 [5, 64, 32, 2048], P(None, 'gx', 'gy', 'gz')
- drag_force: float32 [3, 4, 64, 32, 2048], P(None, None, 'gx', 'gy', 'gz')
The draws below stay inside these ranges and needn't reach their ends.
Inputs may be any that keep to these rules, and one draw needn't show every extreme that they name: `counts`: every cell of the bottom layer holds 4 particles; cells in the lower half of the bed hold up to 4, cells in the upper half up to 2. Slots at or above a cell's count carry no particle.
All inputs are finite; a program needn't handle non-finite values.
Results may differ from the reference program's by a relative error of at most 0.00002.
Values sent between devices are 32-bit elements; how exact they have to be, the bound alone decides.
A program may use at most 128 MiB of HBM per device.

```python
import math
import jax
import jax.numpy as jnp
from jax import lax

SLOTS = 4
ITERS = 4
NX = 64
NY = 32
NZ = 2048


def draw_counts(key, part):
    key = jax.random.fold_in(key, 11)
    key_low, key_high = jax.random.split(key)
    height = lax.broadcasted_iota(jnp.int32, (NX, NY, NZ), 2)
    dense_bed = jax.random.randint(key_low, (NX, NY, NZ), 0, SLOTS + 1)
    sparse_top = jax.random.randint(key_high, (NX, NY, NZ), 0, SLOTS // 2 + 1)
    filled = jnp.where(height < NZ // 2, dense_bed, sparse_top)
    return jnp.where(height == 0, SLOTS, filled).astype(jnp.int32)


def shard_levels(rng, dims, pieces, smallest, high):
    gain = 1.0
    for dim, shards_of in pieces:
        steps = jax.random.uniform(jax.random.fold_in(jax.random.fold_in(rng, 6), dim), (shards_of,), jnp.float32, smallest / len(pieces), high / len(pieces))
        gain = gain * jnp.repeat(jnp.exp(steps), dims[dim] // shards_of).reshape((-1,) + (1,) * (len(dims) - 1 - dim))
    return gain


def noise(own_key, extent, spread, most, pieces=(), kind=jnp.bfloat16):
    result = spread * jax.random.normal(own_key, extent, jnp.float32)
    if pieces:
        result = result * shard_levels(own_key, extent, pieces, -0.22, 0.18)
    return jnp.clip(result, -most, most).astype(kind)


def setup_inputs(seed: int = 0) -> dict:
    seeds = jax.random.split(jax.random.key(seed), 7)
    return {
        "counts": draw_counts(jax.random.fold_in(seeds[6], 71), 0),
        "offsets": jnp.clip(1.0 * jax.random.uniform(seeds[1], (3, SLOTS, NX, NY, NZ), jnp.float32) ** shard_levels(seeds[1], (3, SLOTS, NX, NY, NZ), ((2, 16), (3, 4), (4, 16)), -0.2, 0.2), 0.0, 1.0),
        "volume": jnp.clip(jnp.exp(math.log(0.25) - 2.5257287 * jax.random.uniform(seeds[2], (SLOTS, NX, NY, NZ), jnp.float32) ** shard_levels(seeds[2], (SLOTS, NX, NY, NZ), ((1, 16), (2, 4), (3, 16)), -0.2, 0.2)), 0.02, 0.25),
        "beta": jnp.clip(jnp.exp(math.log(3.0) - 2.3025851 * jax.random.uniform(seeds[3], (SLOTS, NX, NY, NZ), jnp.float32) ** shard_levels(seeds[3], (SLOTS, NX, NY, NZ), ((1, 16), (2, 4), (3, 16)), -0.2, 0.2)), 0.3, 3.0),
        "particle_velocity": noise(seeds[4], (3, SLOTS, NX, NY, NZ), 1.0, 6.0, ((2, 16), (3, 4), (4, 16)), jnp.float32),
        "gas_velocity": noise(seeds[5], (3, NX, NY, NZ), 1.0, 6.0, ((1, 16), (2, 4), (3, 16)), jnp.float32),
    }


SIGMA = 0.6
FILTER = 2.0


def kernel_weights(offset):
    curves = [jnp.exp(-jnp.square(stride + 0.5 - offset) / (2.0 * SIGMA * SIGMA)) for stride in (-1.0, 0.0, 1.0)]
    weight_sum = curves[0] + curves[1] + curves[2]
    return [single / weight_sum for single in curves]


def window_of(first_x, first_y, first_z, size_x, size_y, size_z):
    return (slice(first_x, first_x + size_x), slice(first_y, first_y + size_y), slice(first_z, first_z + size_z))


def neighbour_sum(padded):
    return (padded[:, 2:, 1:-1, 1:-1] + padded[:, :-2, 1:-1, 1:-1] + padded[:, 1:-1, 2:, 1:-1]
            + padded[:, 1:-1, :-2, 1:-1] + padded[:, 1:-1, 1:-1, 2:] + padded[:, 1:-1, 1:-1, :-2])


def deposit_slot(deposit_sum, slot_data):
    slot_sources, slot_offsets = slot_data
    size_x, size_y, size_z = slot_sources.shape[1:]
    padded_sources = jnp.pad(slot_sources, ((0, 0), (1, 1), (1, 1), (1, 1)))
    weight_x = [jnp.pad(single, 1) for single in kernel_weights(slot_offsets[0])]
    weight_y = [jnp.pad(single, 1) for single in kernel_weights(slot_offsets[1])]
    weight_z = [jnp.pad(single, 1) for single in kernel_weights(slot_offsets[2])]
    for index_x in range(3):
        for index_y in range(3):
            for index_z in range(3):
                window = window_of(2 - index_x, 2 - index_y, 2 - index_z, size_x, size_y, size_z)
                factor = weight_x[index_x][window] * weight_y[index_y][window] * weight_z[index_z][window]
                deposit_sum = deposit_sum + padded_sources[(slice(None),) + window] * factor[None]
    return deposit_sum, None


def interpolate_slot(slot_data, gas_padded):
    slot_offsets, slot_beta, slot_velocity, slot_occupied = slot_data
    size_x, size_y, size_z = slot_beta.shape
    weight_x = kernel_weights(slot_offsets[0])
    weight_y = kernel_weights(slot_offsets[1])
    weight_z = kernel_weights(slot_offsets[2])
    gas_at = jnp.zeros((3, size_x, size_y, size_z), jnp.float32)
    for index_x in range(3):
        for index_y in range(3):
            for index_z in range(3):
                window = window_of(index_x, index_y, index_z, size_x, size_y, size_z)
                factor = weight_x[index_x] * weight_y[index_y] * weight_z[index_z]
                gas_at = gas_at + gas_padded[(slice(None),) + window] * factor[None]
    return slot_occupied[None] * slot_beta[None] * (gas_at - slot_velocity)


def reference(counts, offsets, volume, beta, particle_velocity, gas_velocity):
    slot_iota = lax.broadcasted_iota(jnp.int32, (SLOTS,) + counts.shape, 0)
    occupied = (slot_iota < counts[None]).astype(jnp.float32)
    sources = jnp.stack([volume, beta, beta * particle_velocity[0], beta * particle_velocity[1],
                         beta * particle_velocity[2]]) * occupied[None]
    zeros_init = jnp.zeros((5,) + counts.shape, jnp.float32)
    deposited, _ = lax.scan(deposit_slot, zeros_init, (jnp.moveaxis(sources, 1, 0), jnp.moveaxis(offsets, 1, 0)))
    current = deposited
    for sweep_index in range(ITERS):
        padded = jnp.pad(current, ((0, 0), (1, 1), (1, 1), (1, 1)))
        current = (deposited + FILTER * neighbour_sum(padded)) / (1.0 + 6.0 * FILTER)
    gas_padded = jnp.pad(gas_velocity, ((0, 0), (1, 1), (1, 1), (1, 1)))
    forces = lax.map(lambda slot_data: interpolate_slot(slot_data, gas_padded),
                     (jnp.moveaxis(offsets, 1, 0), beta, jnp.moveaxis(particle_velocity, 1, 0), occupied))
    return current, jnp.moveaxis(forces, 0, 1)
```

```python
import functools
import math

import jax
import jax.numpy as jnp
from jax import lax
from jax.experimental import pallas as pl
from jax.experimental.pallas import tpu as pltpu
from jax.sharding import PartitionSpec as P

MESH = pl.DeviceIdType.MESH
F32 = jnp.float32
SIGMA = 0.6
INV_S2 = 1.0 / (SIGMA * SIGMA)
CENTRE = math.exp(0.5 * INV_S2)

DIAG = ((-1, -1), (-1, 1), (1, -1), (1, 1))
ALL = ([(0, a, b) for a in (-1, 0, 1) for b in (-1, 0, 1) if (a, b) != (0, 0)]
       + [(-1, 0, 0), (1, 0, 0), (-2, 0, 0), (2, 0, 0)])


def rot(value, shift, axis):
    size = value.shape[axis]
    return pltpu.roll(value, shift % size, axis)


def kernel(sizes, counts_h, offsets_h, volume_h, beta_h, pv_h, gas_h, filtered_h, drag_h,
           counts_v, offsets_v, src_v, pv_v, gas_v, occ_v, prod_v, shifted_v,
           dm_v, dy_v, dz_v, dyz_v, mx_v, mxy_v,
           sy_v, sz_v, sd_v, ry_v, rz_v, rd_v,
           sgy_v, sgz_v, rgy_v, rgz_v, rgd_v,
           fx_v, fx2_v, rx_v, rx2_v, out_v, drag_v,
           in_sem, out_sem, y_ss, y_rs, z_ss, z_rs, d_ss, d_rs,
           gx_ss, gx_rs, gy_ss, gy_rs, gz_ss, gz_rs, gd_ss, gd_rs, x_ss, x_rs, x2_ss, x2_rs):
    me = (lax.axis_index("gx"), lax.axis_index("gy"), lax.axis_index("gz"))

    def near(step):
        place = tuple(me[i] + step[i] for i in range(3))
        ok = None
        for i in range(3):
            if step[i]:
                inside = (place[i] >= 0) & (place[i] < sizes[i])
                ok = inside if ok is None else ok & inside
        return place, ok

    def send(step, src, dst, ssem, rsem):
        place, ok = near(step)

        @pl.when(ok)
        def _():
            pltpu.make_async_remote_copy(src_ref=src, dst_ref=dst, send_sem=ssem, recv_sem=rsem,
                                         device_id=place, device_id_type=MESH).start()

    def wait_recv(step, src, dst, ssem, rsem):
        place, ok = near(step)

        @pl.when(ok)
        def _():
            pltpu.make_async_remote_copy(src_ref=src, dst_ref=dst, send_sem=ssem, recv_sem=rsem,
                                         device_id=place, device_id_type=MESH).wait_recv()

    def wait_send(step, src, dst, ssem, rsem):
        place, ok = near(step)

        @pl.when(ok)
        def _():
            pltpu.make_async_remote_copy(src_ref=src, dst_ref=dst, send_sem=ssem, recv_sem=rsem,
                                         device_id=place, device_id_type=MESH).wait_send()

    loads = [
        pltpu.make_async_copy(gas_h, gas_v.at[:, pl.ds(1, 4)], in_sem.at[0]),
        pltpu.make_async_copy(counts_h, counts_v, in_sem.at[1]),
        pltpu.make_async_copy(offsets_h, offsets_v, in_sem.at[2]),
        pltpu.make_async_copy(volume_h, src_v.at[0], in_sem.at[3]),
        pltpu.make_async_copy(beta_h, src_v.at[1], in_sem.at[4]),
        pltpu.make_async_copy(pv_h, pv_v, in_sem.at[5]),
    ]
    for load in loads:
        load.start()
    barrier = pltpu.get_barrier_semaphore()
    greeted = jnp.int32(0)
    for step in ALL:
        place, ok = near(step)
        greeted = greeted + ok.astype(jnp.int32)

        @pl.when(ok)
        def _():
            pl.semaphore_signal(barrier, inc=1, device_id=place, device_id_type=MESH)

    def clear(step, refs):
        _, ok = near(step)

        @pl.when(jnp.logical_not(ok))
        def _():
            for ref in refs:
                ref[...] = jnp.zeros(ref.shape, F32)

    for n, s in enumerate((-1, 1)):
        clear((s, 0, 0), [gas_v.at[:, 5 * n], rx_v.at[n]])
        clear((2 * s, 0, 0), [rx2_v.at[n]])
        clear((0, s, 0), [ry_v.at[n], rgy_v.at[n]])
        clear((0, 0, s), [rz_v.at[n], rgz_v.at[n]])
    for n, (a, b) in enumerate(DIAG):
        clear((0, a, b), [rd_v.at[n], rgd_v.at[n]])

    row = lax.broadcasted_iota(jnp.int32, (8, 128), 0)
    lane = lax.broadcasted_iota(jnp.int32, (8, 128), 1)
    slot, col = lane >> 3, lane & 7
    row0, row7, row_low = row == 0, row == 7, row < 4
    lane0, lane127, col_low = lane == 0, lane == 127, col < 4
    col3, col4 = col == 3, col == 4

    coef = F32(2.0 / 13.0)
    plane = lax.broadcasted_iota(jnp.int32, (14, 8, 128), 0) + (4 * me[0] - 5)
    in_x = jnp.where((plane >= 0) & (plane < 4 * sizes[0]), coef, 0.0)
    row_ok = jnp.where(row_low, (me[1] < sizes[1] - 1).astype(F32), (me[1] > 0).astype(F32))
    mx_v[...] = in_x
    mxy_v[...] = in_x * row_ok[None]
    slot_plane = slot + (4 * me[0] - 5)
    cz = jnp.where((slot_plane >= 0) & (slot_plane < 4 * sizes[0]), coef, 0.0) * jnp.where(
        col_low, (me[2] > 0).astype(F32), (me[2] < sizes[2] - 1).astype(F32))
    cyz = cz * row_ok

    loads[0].wait()
    pl.semaphore_wait(barrier, greeted)
    gas_x = [((-1, 0, 0), gas_v.at[:, 1], gas_v.at[:, 5], gx_ss.at[0], gx_rs.at[1]),
             ((1, 0, 0), gas_v.at[:, 4], gas_v.at[:, 0], gx_ss.at[1], gx_rs.at[0])]
    for item in gas_x:
        send(*item)

    loads[1].wait()
    loads[2].wait()

    def products(s, carry):
        occ = jnp.where(counts_v[...] > s, F32(1.0), F32(0.0))
        occ_v[s] = occ
        weights, norm = [], None
        for axis in range(3):
            t = jnp.exp((0.5 - offsets_v[axis, s]) * INV_S2)
            low, mid = t * t, CENTRE * t
            total = low + mid + 1.0
            norm = total if norm is None else norm * total
            weights.append((low, mid))
        scale = occ / norm
        wx = (weights[0][0] * scale, weights[0][1] * scale, scale)
        for a in range(3):
            for b in range(3):
                xy = wx[a] * weights[1][b] if b < 2 else wx[a]
                for c in range(3):
                    prod_v[9 * a + 3 * b + c, s] = xy * weights[2][c] if c < 2 else xy
        return carry

    lax.fori_loop(0, 4, products, 0)
    for load in loads[3:]:
        load.wait()
    for j in range(3):
        src_v[2 + j] = src_v[1] * pv_v[j]

    def pack(planes, first):
        result = jnp.zeros((8, 128), F32)
        for i in range(planes.shape[0]):
            result = jnp.where(slot == first + i, rot(planes[i], 8 * (first + i) + 4, 1), result)
        return result

    def unpack(tile, first, count):
        return jnp.stack([rot(tile, -(8 * (first + i) + 4), 1) for i in range(count)])

    def y_copy(n, k):
        return ((0, (-1, 1)[n], 0), sy_v.at[n, k], ry_v.at[1 - n, k], y_ss.at[n, k], y_rs.at[1 - n, k])

    def deposit(k, carry):
        src = [src_v[k, s] for s in range(4)]
        mz, zz = [], []
        for b in range(3):
            by_z = []
            for c in range(3):
                by_x = []
                for a in range(3):
                    total = src[0] * prod_v[9 * a + 3 * b + c, 0]
                    for s in range(1, 4):
                        total = total + src[s] * prod_v[9 * a + 3 * b + c, s]
                    by_x.append(total)
                lo, mid, hi = by_x
                by_z.append(jnp.concatenate([
                    lo[0:1], lo[1:2] + mid[0:1], lo[2:4] + mid[1:3] + hi[0:2], mid[3:4] + hi[2:3], hi[3:4]], axis=0))
            up, down = rot(by_z[2], 1, 2), rot(by_z[0], -1, 2)
            mz.append(by_z[1] + jnp.where(lane0[None], 0.0, up) + jnp.where(lane127[None], 0.0, down))
            spill = jnp.where(lane0[None], up, jnp.where(lane127[None], down, 0.0))
            packed = rot(spill[0], 36, 1)
            for i in range(1, 6):
                packed = packed + rot(spill[i], 8 * i + 36, 1)
            zz.append(packed)
        up, down = rot(mz[2], 1, 1), rot(mz[0], -1, 1)
        m = mz[1] + jnp.where(row0[None], 0.0, up) + jnp.where(row7[None], 0.0, down)
        y = jnp.where(row0[None], up, jnp.where(row7[None], down, 0.0))
        up, down = rot(zz[2], 1, 0), rot(zz[0], -1, 0)
        z = zz[1] + jnp.where(row0, 0.0, up) + jnp.where(row7, 0.0, down)
        yz = jnp.where(row0, up, jnp.where(row7, down, 0.0))
        dm_v[k], dy_v[k], dz_v[k], dyz_v[k] = m, y, z, yz
        sy_v[0, k, 0:6] = jnp.where(row_low[None], m, y)
        sy_v[1, k, 0:6] = jnp.where(row_low[None], y, m)
        sy_v[0, k, 6] = jnp.where(row_low, z, yz)
        sy_v[1, k, 6] = jnp.where(row_low, yz, z)
        for n in range(2):
            send(*y_copy(n, k))
        mp, yp = pack(m, 4), pack(y, 4)
        zm = (jnp.where(col_low, z, mp), jnp.where(col_low, mp, z))
        zy = (jnp.where(col_low, yz, yp), jnp.where(col_low, yp, yz))
        for n in range(2):
            sz_v[n, k, 0], sz_v[n, k, 1] = zm[n], zy[n]
        for n, (a, b) in enumerate(DIAG):
            first, second = (zm, zy) if a < 0 else (zy, zm)
            sd_v[n, k] = jnp.where(row_low, first[(b + 1) // 2], second[(b + 1) // 2])
        return carry

    lax.fori_loop(0, 5, deposit, 0)
    z_copies = [((0, 0, s), sz_v.at[n], rz_v.at[1 - n], z_ss.at[n], z_rs.at[1 - n]) for n, s in enumerate((-1, 1))]
    d_copies = [((0, a, b), sd_v.at[n], rd_v.at[3 - n], d_ss.at[n], d_rs.at[3 - n]) for n, (a, b) in enumerate(DIAG)]
    for item in d_copies + z_copies:
        send(*item)

    for item in gas_x:
        wait_recv(item[0], item[1], gas_v.at[:, 0 if item[0][0] < 0 else 5], item[3], gx_rs.at[0 if item[0][0] < 0 else 1])
    for j in range(3):
        sgz_v[j] = pack(gas_v[j], 4)
        for i in range(6):
            sgy_v[0, j, pl.ds(i, 1), :] = gas_v[j, i, pl.ds(0, 1), :]
            sgy_v[1, j, pl.ds(i, 1), :] = gas_v[j, i, pl.ds(7, 1), :]
        for n in range(2):
            sgy_v[n, j, pl.ds(6, 2), :] = jnp.zeros((2, 128), F32)
    gy_copies = [((0, s, 0), sgy_v.at[n], rgy_v.at[1 - n], gy_ss.at[n], gy_rs.at[1 - n]) for n, s in enumerate((-1, 1))]
    gz_copies = [((0, 0, s), sgz_v, rgz_v.at[1 - n], gz_ss.at[n], gz_rs.at[1 - n]) for n, s in enumerate((-1, 1))]
    gd_copies = [((0, a, b), sgz_v, rgd_v.at[3 - n], gd_ss.at[n], gd_rs.at[3 - n]) for n, (a, b) in enumerate(DIAG)]
    for item in gy_copies + gz_copies + gd_copies:
        send(*item)

    for n, s in enumerate((-1, 1)):
        wait_recv((0, 0, s), sz_v.at[n], rz_v.at[n], z_ss.at[n], z_rs.at[n])
    for n, (a, b) in enumerate(DIAG):
        wait_recv((0, a, b), sd_v.at[n], rd_v.at[n], d_ss.at[n], d_rs.at[n])

    def x_copies(k):
        return [((-1, 0, 0), fx_v.at[0, k], rx_v.at[1, k], x_ss.at[0, k], x_rs.at[1, k]),
                ((1, 0, 0), fx_v.at[1, k], rx_v.at[0, k], x_ss.at[1, k], x_rs.at[0, k]),
                ((-2, 0, 0), fx2_v.at[0, k], rx2_v.at[1, k], x2_ss.at[0, k], x2_rs.at[1, k]),
                ((2, 0, 0), fx2_v.at[1, k], rx2_v.at[0, k], x2_ss.at[1, k], x2_rs.at[0, k])]

    def widen(cur):
        count = cur.shape[0]
        return jnp.concatenate([cur[0:1], cur[1:2], cur[0:count - 2] + cur[2:count],
                                cur[count - 2:count - 1], cur[count - 1:count]], axis=0)

    def z_sum(tiles, halo, first):
        edge = unpack(halo, first, tiles.shape[0])
        return (rot(jnp.where(lane0[None], edge, tiles), -1, 2) + rot(jnp.where(lane127[None], edge, tiles), 1, 2))

    def y_sum(tiles, halo):
        axis = tiles.ndim - 2
        return rot(jnp.where(row0, halo, tiles), -1, axis) + rot(jnp.where(row7, halo, tiles), 1, axis)

    def packed_sum(tile, edges):
        return (rot(tile, 8, 1) + rot(tile, -8, 1) + rot(jnp.where(col4, edges, tile), -1, 1)
                + rot(jnp.where(col3, edges, tile), 1, 1))

    def grow(total, inner):
        count = total.shape[0]
        return jnp.concatenate([total[0:1], total[1:count - 1] + inner, total[count - 1:count]], axis=0)

    def add_source(total, source, lead):
        count = total.shape[0]
        return jnp.concatenate([total[0:lead], total[lead:lead + 6] + source, total[lead + 6:count]], axis=0)

    def filter_one(k, carry):
        for n in range(2):
            s = (-1, 1)[n]
            wait_recv((0, s, 0), sy_v.at[n, k], ry_v.at[n, k], y_ss.at[n, k], y_rs.at[n, k])
        below, above = ry_v[0, k, 0:6], ry_v[1, k, 0:6]
        below_z, above_z = ry_v[0, k, 6], ry_v[1, k, 6]
        m = dm_v[k] + jnp.where(row_low[None], below, above)
        y = dy_v[k] + jnp.where(row_low[None], above, below)
        side = []
        for n, b in enumerate((0, 1)):
            lower, upper = rd_v[b, k], rd_v[2 + b, k]
            side.append((rz_v[n, k, 0] + jnp.where(row_low, lower, upper),
                         rz_v[n, k, 1] + jnp.where(row_low, upper, lower)))
        z = dz_v[k] + jnp.where(col_low, side[0][0], side[1][0]) + jnp.where(row_low, below_z, above_z)
        yz = dyz_v[k] + jnp.where(col_low, side[0][1], side[1][1]) + jnp.where(row_low, above_z, below_z)
        ends = (lane0 | lane127)[None]
        m = m + jnp.where(ends, unpack(jnp.where(col_low, side[1][0], side[0][0]), 4, 6), 0.0)
        y = y + jnp.where(ends, unpack(jnp.where(col_low, side[1][1], side[0][1]), 4, 6), 0.0)
        m13, y13 = m * (0.5 * mx_v[4:10]), y * (0.5 * mxy_v[4:10])
        z13, yz13 = z * (0.5 * cz), yz * (0.5 * cyz)
        cm, cy, cz_now, cyz_now = m13, y13, z13, yz13
        for sweep in range(1, 5):
            first = 5 - sweep
            gain = F32(13.0) if sweep == 1 else None
            scale_m = mx_v[first - 1:first + 5 + 2 * sweep]
            m_sum = grow(widen(cm), y_sum(cm, cy) + z_sum(cm, cz_now, first))
            if gain is not None:
                m_sum = m_sum * gain
            next_m = add_source(m_sum * scale_m, m13, sweep)
            if sweep < 4:
                scale_y = mxy_v[first - 1:first + 5 + 2 * sweep]
                y_total = grow(widen(cy), y_sum(cy, cm) + z_sum(cy, cyz_now, first))
                z_total = packed_sum(cz_now, pack(cm, first)) + y_sum(cz_now, cyz_now)
                yz_total = packed_sum(cyz_now, pack(cy, first)) + y_sum(cyz_now, cz_now)
                if gain is not None:
                    y_total, z_total, yz_total = y_total * gain, z_total * gain, yz_total * gain
                cy = add_source(y_total * scale_y, y13, sweep)
                cz_now, cyz_now = z13 + z_total * cz, yz13 + yz_total * cyz
            cm = next_m
        fx2_v[0, k] = cm[0]
        fx_v[0, k] = cm[1:5]
        out_v[k] = cm[5:9]
        fx_v[1, k] = cm[9:13]
        fx2_v[1, k] = cm[13]
        for item in x_copies(k):
            send(*item)
        return carry

    lax.fori_loop(0, 5, filter_one, 0)

    for n, s in enumerate((-1, 1)):
        wait_recv((0, s, 0), sgy_v.at[n], rgy_v.at[n], gy_ss.at[n], gy_rs.at[n])
        wait_recv((0, 0, s), sgz_v, rgz_v.at[n], gz_ss.at[n], gz_rs.at[n])
    for n, (a, b) in enumerate(DIAG):
        wait_recv((0, a, b), sgz_v, rgd_v.at[n], gd_ss.at[n], gd_rs.at[n])

    def shift(j, carry):
        tiles = gas_v[j]
        below, above = rgy_v[0, j], rgy_v[1, j]
        rows = jnp.stack([jnp.where(row0, jnp.broadcast_to(above[i:i + 1], (8, 128)),
                                    jnp.broadcast_to(below[i:i + 1], (8, 128))) for i in range(6)])
        halo_m = jnp.where(col_low, rgz_v[0, j], rgz_v[1, j])
        halo_y = jnp.where(col_low, jnp.where(row0, rgd_v[2, j], rgd_v[0, j]),
                           jnp.where(row0, rgd_v[3, j], rgd_v[1, j]))
        variants = []
        for value, halo in ((tiles, halo_m), (rows, halo_y)):
            edge = unpack(halo, 4, 6)
            variants.append((rot(jnp.where(lane127[None], edge, value), 1, 2), value,
                             rot(jnp.where(lane0[None], edge, value), -1, 2)))
        for c in range(3):
            value, halo = variants[0][c], variants[1][c]
            shifted_v[j, c] = rot(jnp.where(row7[None], halo, value), 1, 1)
            shifted_v[j, 3 + c] = value
            shifted_v[j, 6 + c] = rot(jnp.where(row0[None], halo, value), -1, 1)
        return carry

    lax.fori_loop(0, 3, shift, 0)

    def drag(x, carry):
        totals = [jnp.zeros((4, 8, 128), F32) for _ in range(3)]
        for a in range(3):
            for bc in range(9):
                weight = prod_v[9 * a + bc, :, x]
                for j in range(3):
                    totals[j] = totals[j] + weight * shifted_v[j, bc, x + a][None]
        for j in range(3):
            drag_v[j, :, x] = src_v[1, :, x] * totals[j] - occ_v[:, x] * src_v[2 + j, :, x]
        return carry

    lax.fori_loop(0, 4, drag, 0)
    drag_out = pltpu.make_async_copy(drag_v, drag_h, out_sem.at[0])
    drag_out.start()

    def finish(k, carry):
        for n in range(2):
            s = (-1, 1)[n]
            wait_recv((s, 0, 0), fx_v.at[n, k], rx_v.at[n, k], x_ss.at[n, k], x_rs.at[n, k])
            wait_recv((2 * s, 0, 0), fx2_v.at[n, k], rx2_v.at[n, k], x2_ss.at[n, k], x2_rs.at[n, k])
        total = out_v[k] + (rx_v[0, k] + rx_v[1, k])
        out_v[k] = jnp.concatenate([total[0:1] + rx2_v[0, k][None], total[1:3], total[3:4] + rx2_v[1, k][None]], axis=0)
        return carry

    lax.fori_loop(0, 5, finish, 0)
    filtered_out = pltpu.make_async_copy(out_v, filtered_h, out_sem.at[1])
    filtered_out.start()

    def sent(k, carry):
        for n in range(2):
            wait_send(*y_copy(n, k))
        for item in x_copies(k):
            wait_send(*item)
        return carry

    lax.fori_loop(0, 5, sent, 0)
    for item in gas_x + z_copies + d_copies + gy_copies + gz_copies + gd_copies:
        wait_send(*item)
    drag_out.wait()
    filtered_out.wait()


def solution(mesh):
    sizes = tuple(mesh.shape[name] for name in ("gx", "gy", "gz"))
    dma = pltpu.SemaphoreType.DMA

    def vmem(*shape):
        return pltpu.VMEM(shape + (8, 128), F32)

    def shards(counts, offsets, volume, beta, particle_velocity, gas_velocity):
        any_space = pl.BlockSpec(memory_space=pl.ANY)
        return pl.pallas_call(
            functools.partial(kernel, sizes),
            out_shape=(jax.ShapeDtypeStruct((5, 4, 8, 128), F32), jax.ShapeDtypeStruct((3, 4, 4, 8, 128), F32)),
            in_specs=[any_space] * 6,
            out_specs=(any_space, any_space),
            scratch_shapes=[
                pltpu.VMEM((4, 8, 128), jnp.int32), vmem(3, 4, 4), vmem(5, 4, 4), vmem(3, 4, 4), vmem(3, 6),
                vmem(4, 4), vmem(27, 4, 4), vmem(3, 9, 6),
                vmem(5, 6), vmem(5, 6), vmem(5), vmem(5), vmem(14), vmem(14),
                vmem(2, 5, 7), vmem(2, 5, 2), vmem(4, 5), vmem(2, 5, 7), vmem(2, 5, 2), vmem(4, 5),
                vmem(2, 3), vmem(3), vmem(2, 3), vmem(2, 3), vmem(4, 3),
                vmem(2, 5, 4), vmem(2, 5), vmem(2, 5, 4), vmem(2, 5), vmem(5, 4), vmem(3, 4, 4),
                dma((6,)), dma((2,)), dma((2, 5)), dma((2, 5)), dma((2,)), dma((2,)), dma((4,)), dma((4,)),
                dma((2,)), dma((2,)), dma((2,)), dma((2,)), dma((2,)), dma((2,)), dma((4,)), dma((4,)),
                dma((2, 5)), dma((2, 5)), dma((2, 5)), dma((2, 5)),
            ],
            compiler_params=pltpu.CompilerParams(
                collective_id=0, has_side_effects=True, vmem_limit_bytes=32 * 2**20),
            name="deposit_filter_drag",
        )(counts, offsets, volume, beta, particle_velocity, gas_velocity)

    in_specs = (
        P("gx", "gy", "gz"),
        P(None, None, "gx", "gy", "gz"),
        P(None, "gx", "gy", "gz"),
        P(None, "gx", "gy", "gz"),
        P(None, None, "gx", "gy", "gz"),
        P(None, "gx", "gy", "gz"),
    )
    out_specs = (P(None, "gx", "gy", "gz"), P(None, None, "gx", "gy", "gz"))
    return jax.shard_map(shards, mesh=mesh, in_specs=in_specs, out_specs=out_specs, check_vma=False)
```

```python
import functools
import math

import jax
import jax.numpy as jnp
import numpy as np
from jax import lax
from jax.experimental import pallas as pl
from jax.experimental.pallas import tpu as pltpu
from jax.sharding import PartitionSpec as P

MESH = pl.DeviceIdType.MESH
F32 = jnp.float32
SIGMA = 0.6
INV_S2 = 1.0 / (SIGMA * SIGMA)
CENTRE = math.exp(0.5 * INV_S2)
ITERS = 4
FILTER = 2.0

DIAG = ((-1, -1), (-1, 1), (1, -1), (1, 1))
ALL = ([(0, a, b) for a in (-1, 0, 1) for b in (-1, 0, 1) if (a, b) != (0, 0)]
       + [(-1, 0, 0), (1, 0, 0), (-2, 0, 0), (2, 0, 0)])


def filter_taps():
    unit = np.zeros((2 * ITERS + 3,) * 3)
    unit[(ITERS + 1,) * 3] = 1.0
    current = unit
    for _ in range(ITERS):
        around = sum(np.roll(current, step, axis) for axis in range(3) for step in (-1, 1))
        current = (unit + FILTER * around) / (1.0 + 6.0 * FILTER)
    return current[ITERS + 1:, ITERS + 1:, ITERS + 1:]


TAPS = filter_taps()


def rot(value, shift, axis):
    size = value.shape[axis]
    return pltpu.roll(value, shift % size, axis)


def kernel(sizes, counts_h, offsets_h, volume_h, beta_h, pv_h, gas_h, filtered_h, drag_h,
           counts_v, offsets_v, src_v, pv_v, gas_v, occ_v, prod_v, shifted_v,
           dm_v, dy_v, dz_v, dyz_v,
           sy_v, sz_v, sd_v, ry_v, rz_v, rd_v,
           sgy_v, sgz_v, rgy_v, rgz_v, rgd_v,
           fx_v, fx2_v, rx_v, rx2_v, out_v, drag_v,
           in_sem, out_sem, y_ss, y_rs, z_ss, z_rs, d_ss, d_rs,
           gx_ss, gx_rs, gy_ss, gy_rs, gz_ss, gz_rs, gd_ss, gd_rs, x_ss, x_rs, x2_ss, x2_rs):
    me = (lax.axis_index("gx"), lax.axis_index("gy"), lax.axis_index("gz"))

    def near(step):
        place = tuple(me[i] + step[i] for i in range(3))
        ok = None
        for i in range(3):
            if step[i]:
                inside = (place[i] >= 0) & (place[i] < sizes[i])
                ok = inside if ok is None else ok & inside
        return place, ok

    def send(step, src, dst, ssem, rsem):
        place, ok = near(step)

        @pl.when(ok)
        def _():
            pltpu.make_async_remote_copy(src_ref=src, dst_ref=dst, send_sem=ssem, recv_sem=rsem,
                                         device_id=place, device_id_type=MESH).start()

    def wait_recv(step, src, dst, ssem, rsem):
        place, ok = near(step)

        @pl.when(ok)
        def _():
            pltpu.make_async_remote_copy(src_ref=src, dst_ref=dst, send_sem=ssem, recv_sem=rsem,
                                         device_id=place, device_id_type=MESH).wait_recv()

    def wait_send(step, src, dst, ssem, rsem):
        place, ok = near(step)

        @pl.when(ok)
        def _():
            pltpu.make_async_remote_copy(src_ref=src, dst_ref=dst, send_sem=ssem, recv_sem=rsem,
                                         device_id=place, device_id_type=MESH).wait_send()

    loads = [
        pltpu.make_async_copy(gas_h, gas_v.at[:, pl.ds(1, 4)], in_sem.at[0]),
        pltpu.make_async_copy(counts_h, counts_v, in_sem.at[1]),
        pltpu.make_async_copy(offsets_h, offsets_v, in_sem.at[2]),
        pltpu.make_async_copy(volume_h, src_v.at[0], in_sem.at[3]),
        pltpu.make_async_copy(beta_h, src_v.at[1], in_sem.at[4]),
        pltpu.make_async_copy(pv_h, pv_v, in_sem.at[5]),
    ]
    for load in loads:
        load.start()
    barrier = pltpu.get_barrier_semaphore()
    greeted = jnp.int32(0)
    for step in ALL:
        place, ok = near(step)
        greeted = greeted + ok.astype(jnp.int32)

        @pl.when(ok)
        def _():
            pl.semaphore_signal(barrier, inc=1, device_id=place, device_id_type=MESH)

    def clear(step, refs):
        _, ok = near(step)

        @pl.when(jnp.logical_not(ok))
        def _():
            for ref in refs:
                ref[...] = jnp.zeros(ref.shape, F32)

    for n, s in enumerate((-1, 1)):
        clear((s, 0, 0), [gas_v.at[:, 5 * n], rx_v.at[n]])
        clear((2 * s, 0, 0), [rx2_v.at[n]])
        clear((0, s, 0), [ry_v.at[n], rgy_v.at[n]])
        clear((0, 0, s), [rz_v.at[n], rgz_v.at[n]])
    for n, (a, b) in enumerate(DIAG):
        clear((0, a, b), [rd_v.at[n], rgd_v.at[n]])

    row = lax.broadcasted_iota(jnp.int32, (8, 128), 0)
    lane = lax.broadcasted_iota(jnp.int32, (8, 128), 1)
    slot, col = lane >> 3, lane & 7
    row0, row7, row_low = row == 0, row == 7, row < 4
    lane0, lane127, col_low = lane == 0, lane == 127, col < 4
    col3, col4 = col == 3, col == 4

    edge_rows = (row_low & (me[1] == sizes[1] - 1)) | (~row_low & (me[1] == 0))
    edge_cols = (col_low & (me[2] == 0)) | (~col_low & (me[2] == sizes[2] - 1))
    keep_first, keep_last = (me[0] > 0).astype(F32), (me[0] < sizes[0] - 1).astype(F32)

    def mirror_rows(tiles, spill):
        image = jnp.where((row == 1) | (row == 4), rot(tiles, 2, tiles.ndim - 2), jnp.where(
            (row == 2) | (row == 5), rot(tiles, 4, tiles.ndim - 2),
            jnp.where((row == 3) | (row == 6), rot(tiles, 6, tiles.ndim - 2), 0.0)))
        return jnp.where(edge_rows, -image, spill)

    def mirror_cols(packed, spill):
        image = jnp.where(col == 0, rot(packed, -6, 1), jnp.where(col == 1, rot(packed, -4, 1), jnp.where(
            col == 2, rot(packed, -2, 1), jnp.where(col == 5, rot(packed, 2, 1), jnp.where(
                col == 6, rot(packed, 4, 1), jnp.where(col == 7, rot(packed, 6, 1), 0.0))))))
        return jnp.where(edge_cols, -image, spill)

    enters_last = (me[0] == 0) & (me[1] == 0) & (me[2] == 0)
    loads[0].wait()
    gas_x = [((-1, 0, 0), gas_v.at[:, 1], gas_v.at[:, 5], gx_ss.at[0], gx_rs.at[1]),
             ((1, 0, 0), gas_v.at[:, 4], gas_v.at[:, 0], gx_ss.at[1], gx_rs.at[0])]

    @pl.when(enters_last)
    def _():
        pl.semaphore_wait(barrier, greeted)
        for item in gas_x:
            send(*item)

    loads[1].wait()
    loads[2].wait()

    def products(s, carry):
        occ = jnp.where(counts_v[...] > s, F32(1.0), F32(0.0))
        occ_v[s] = occ
        weights, norm = [], None
        for axis in range(3):
            t = jnp.exp((0.5 - offsets_v[axis, s]) * INV_S2)
            low, mid = t * t, CENTRE * t
            total = low + mid + 1.0
            norm = total if norm is None else norm * total
            weights.append((low, mid))
        scale = occ / norm
        wx = (weights[0][0] * scale, weights[0][1] * scale, scale)
        for a in range(3):
            for b in range(3):
                xy = wx[a] * weights[1][b] if b < 2 else wx[a]
                for c in range(3):
                    prod_v[9 * a + 3 * b + c, s] = xy * weights[2][c] if c < 2 else xy
        return carry

    lax.fori_loop(0, 4, products, 0)
    for load in loads[3:]:
        load.wait()
    for j in range(3):
        src_v[2 + j] = src_v[1] * pv_v[j]

    def pack(planes, first):
        result = jnp.zeros((8, 128), F32)
        for i in range(planes.shape[0]):
            result = jnp.where(slot == first + i, rot(planes[i], 8 * (first + i) + 4, 1), result)
        return result

    def unpack(tile, first, count):
        return jnp.stack([rot(tile, -(8 * (first + i) + 4), 1) for i in range(count)])

    def y_copy(n, k):
        return ((0, (-1, 1)[n], 0), sy_v.at[n, k], ry_v.at[1 - n, k], y_ss.at[n, k], y_rs.at[1 - n, k])

    def deposit(k, carry):
        src = [src_v[k, s] for s in range(4)]
        by_z = []
        for c in range(3):
            by_y = []
            for b in range(3):
                by_x = []
                for a in range(3):
                    total = src[0] * prod_v[9 * a + 3 * b + c, 0]
                    for s in range(1, 4):
                        total = total + src[s] * prod_v[9 * a + 3 * b + c, s]
                    by_x.append(total)
                lo, mid, hi = by_x
                by_y.append(jnp.concatenate([
                    lo[0:1], lo[1:2] + mid[0:1], lo[2:4] + mid[1:3] + hi[0:2], mid[3:4] + hi[2:3], hi[3:4]], axis=0))
            up, down = rot(by_y[2], 1, 1), rot(by_y[0], -1, 1)
            by_z.append((by_y[1] + jnp.where(row0, 0.0, up) + jnp.where(row7, 0.0, down),
                         jnp.where(row0, up, jnp.where(row7, down, 0.0))))
        main, packs = [], []
        for kind in range(2):
            up, down = rot(by_z[2][kind], 1, 2), rot(by_z[0][kind], -1, 2)
            spill = jnp.where(lane0, up, jnp.where(lane127, down, 0.0))
            main.append(by_z[1][kind] + jnp.where(lane0, 0.0, up) + jnp.where(lane127, 0.0, down))
            packed = rot(spill[0], 36, 1) * keep_first
            for i in range(1, 5):
                packed = packed + rot(spill[i], 8 * i + 36, 1)
            packs.append(packed + rot(spill[5], 76, 1) * keep_last)
        m, y = [jnp.concatenate([v[0:1] * keep_first, v[1:5], v[5:6] * keep_last], axis=0) for v in main]
        z, yz = packs
        y, yz = mirror_rows(m, y), mirror_rows(z, yz)
        mp, yp = pack(m, 4), pack(y, 4)
        z, yz = mirror_cols(mp, z), mirror_cols(yp, yz)
        dm_v[k], dy_v[k], dz_v[k], dyz_v[k] = m, y, z, yz
        sy_v[0, k, 0:6] = jnp.where(row_low, m, y)
        sy_v[1, k, 0:6] = jnp.where(row_low, y, m)
        sy_v[0, k, 6] = jnp.where(row_low, z, yz)
        sy_v[1, k, 6] = jnp.where(row_low, yz, z)
        zm = (jnp.where(col_low, z, mp), jnp.where(col_low, mp, z))
        zy = (jnp.where(col_low, yz, yp), jnp.where(col_low, yp, yz))
        for n in range(2):
            sz_v[n, k, 0], sz_v[n, k, 1] = zm[n], zy[n]
        for n, (a, b) in enumerate(DIAG):
            first, second = (zm, zy) if a < 0 else (zy, zm)
            sd_v[n, k] = jnp.where(row_low, first[(b + 1) // 2], second[(b + 1) // 2])
        return carry

    lax.fori_loop(0, 5, deposit, 0)

    @pl.when(jnp.logical_not(enters_last))
    def _():
        pl.semaphore_wait(barrier, greeted)
        for item in gas_x:
            send(*item)

    def send_y(k, carry):
        for n in range(2):
            send(*y_copy(n, k))
        return carry

    lax.fori_loop(0, 5, send_y, 0)
    z_copies = [((0, 0, s), sz_v.at[n], rz_v.at[1 - n], z_ss.at[n], z_rs.at[1 - n]) for n, s in enumerate((-1, 1))]
    d_copies = [((0, a, b), sd_v.at[n], rd_v.at[3 - n], d_ss.at[n], d_rs.at[3 - n]) for n, (a, b) in enumerate(DIAG)]
    for item in d_copies + z_copies:
        send(*item)

    for item in gas_x:
        wait_recv(item[0], item[1], gas_v.at[:, 0 if item[0][0] < 0 else 5], item[3], gx_rs.at[0 if item[0][0] < 0 else 1])
    for j in range(3):
        sgz_v[j] = pack(gas_v[j], 4)
        for i in range(6):
            sgy_v[0, j, pl.ds(i, 1), :] = gas_v[j, i, pl.ds(0, 1), :]
            sgy_v[1, j, pl.ds(i, 1), :] = gas_v[j, i, pl.ds(7, 1), :]
        for n in range(2):
            sgy_v[n, j, pl.ds(6, 2), :] = jnp.zeros((2, 128), F32)
    gy_copies = [((0, s, 0), sgy_v.at[n], rgy_v.at[1 - n], gy_ss.at[n], gy_rs.at[1 - n]) for n, s in enumerate((-1, 1))]
    gz_copies = [((0, 0, s), sgz_v, rgz_v.at[1 - n], gz_ss.at[n], gz_rs.at[1 - n]) for n, s in enumerate((-1, 1))]
    gd_copies = [((0, a, b), sgz_v, rgd_v.at[3 - n], gd_ss.at[n], gd_rs.at[3 - n]) for n, (a, b) in enumerate(DIAG)]
    for item in gy_copies + gz_copies + gd_copies:
        send(*item)

    for n, s in enumerate((-1, 1)):
        wait_recv((0, 0, s), sz_v.at[n], rz_v.at[n], z_ss.at[n], z_rs.at[n])
    for n, (a, b) in enumerate(DIAG):
        wait_recv((0, a, b), sd_v.at[n], rd_v.at[n], d_ss.at[n], d_rs.at[n])

    def x_copies(k):
        return [((-1, 0, 0), fx_v.at[0, k], rx_v.at[1, k], x_ss.at[0, k], x_rs.at[1, k]),
                ((1, 0, 0), fx_v.at[1, k], rx_v.at[0, k], x_ss.at[1, k], x_rs.at[0, k]),
                ((-2, 0, 0), fx2_v.at[0, k], rx2_v.at[1, k], x2_ss.at[0, k], x2_rs.at[1, k]),
                ((2, 0, 0), fx2_v.at[1, k], rx2_v.at[0, k], x2_ss.at[1, k], x2_rs.at[0, k])]

    def filter_one(k, carry):
        for n in range(2):
            s = (-1, 1)[n]
            wait_recv((0, s, 0), sy_v.at[n, k], ry_v.at[n, k], y_ss.at[n, k], y_rs.at[n, k])
        below, above = ry_v[0, k, 0:6], ry_v[1, k, 0:6]
        below_z, above_z = ry_v[0, k, 6], ry_v[1, k, 6]
        m = dm_v[k] + jnp.where(row_low[None], below, above)
        y = dy_v[k] + jnp.where(row_low[None], above, below)
        side = []
        for n, b in enumerate((0, 1)):
            lower, upper = rd_v[b, k], rd_v[2 + b, k]
            side.append((rz_v[n, k, 0] + jnp.where(row_low, lower, upper),
                         rz_v[n, k, 1] + jnp.where(row_low, upper, lower)))
        z = dz_v[k] + jnp.where(col_low, side[0][0], side[1][0]) + jnp.where(row_low, below_z, above_z)
        yz = dyz_v[k] + jnp.where(col_low, side[0][1], side[1][1]) + jnp.where(row_low, above_z, below_z)
        ends = (lane0 | lane127)[None]
        m = m + jnp.where(ends, unpack(jnp.where(col_low, side[1][0], side[0][0]), 4, 6), 0.0)
        y = y + jnp.where(ends, unpack(jnp.where(col_low, side[1][1], side[0][1]), 4, 6), 0.0)
        edge_m, edge_y = unpack(z, 4, 6), unpack(yz, 4, 6)
        pushed = [None] * 14
        for i in range(6):
            parts = [None] * 5

            def add(sum_s, sum_c, value):
                for d in range(5 - sum_s - sum_c):
                    term = value * F32(TAPS[d, sum_s, sum_c])
                    parts[d] = term if parts[d] is None else parts[d] + term

            for c in range(5):
                rows = []
                for kind, (tile, edge) in enumerate(((m[i], edge_m[i]), (y[i], edge_y[i]))):
                    if c and not (kind and c == 4):
                        tile = (rot(jnp.where(lane < c, edge, tile), -c, 1)
                                + rot(jnp.where(lane >= 128 - c, edge, tile), c, 1))
                    rows.append(tile)
                add(0, c, rows[0])
                for s in range(1, 5 - c):
                    add(s, c, rot(jnp.where(row < s, rows[1], rows[0]), -s, 0)
                        + rot(jnp.where(row >= 8 - s, rows[1], rows[0]), s, 0))
            for d in range(5):
                for q in {i + 4 - d, i + 4 + d}:
                    pushed[q] = parts[d] if pushed[q] is None else pushed[q] + parts[d]
        for n, target in enumerate((fx_v.at[0, k], out_v.at[k], fx_v.at[1, k])):
            for i in range(4):
                target[i] = pushed[1 + 4 * n + i]
        fx2_v[0, k] = pushed[0]
        fx2_v[1, k] = pushed[13]

        @pl.when(me[0] == 0)
        def _():
            for i in range(3):
                rx_v[0, k, i] = -pushed[3 - i]

        @pl.when(me[0] == sizes[0] - 1)
        def _():
            for i in range(1, 4):
                rx_v[1, k, i] = -pushed[13 - i]
        for item in x_copies(k):
            send(*item)
        return carry

    lax.fori_loop(0, 5, filter_one, 0)

    for n, s in enumerate((-1, 1)):
        wait_recv((0, s, 0), sgy_v.at[n], rgy_v.at[n], gy_ss.at[n], gy_rs.at[n])
        wait_recv((0, 0, s), sgz_v, rgz_v.at[n], gz_ss.at[n], gz_rs.at[n])
    for n, (a, b) in enumerate(DIAG):
        wait_recv((0, a, b), sgz_v, rgd_v.at[n], gd_ss.at[n], gd_rs.at[n])

    def shift(j, carry):
        tiles = gas_v[j]
        below, above = rgy_v[0, j], rgy_v[1, j]
        rows = jnp.stack([jnp.where(row0, jnp.broadcast_to(above[i:i + 1], (8, 128)),
                                    jnp.broadcast_to(below[i:i + 1], (8, 128))) for i in range(6)])
        halo_m = jnp.where(col_low, rgz_v[0, j], rgz_v[1, j])
        halo_y = jnp.where(col_low, jnp.where(row0, rgd_v[2, j], rgd_v[0, j]),
                           jnp.where(row0, rgd_v[3, j], rgd_v[1, j]))
        variants = []
        for value, halo in ((tiles, halo_m), (rows, halo_y)):
            edge = unpack(halo, 4, 6)
            variants.append((rot(jnp.where(lane127[None], edge, value), 1, 2), value,
                             rot(jnp.where(lane0[None], edge, value), -1, 2)))
        for c in range(3):
            value, halo = variants[0][c], variants[1][c]
            shifted_v[j, c] = rot(jnp.where(row7[None], halo, value), 1, 1)
            shifted_v[j, 3 + c] = value
            shifted_v[j, 6 + c] = rot(jnp.where(row0[None], halo, value), -1, 1)
        return carry

    lax.fori_loop(0, 3, shift, 0)

    def drag(x, carry):
        totals = [jnp.zeros((4, 8, 128), F32) for _ in range(3)]
        for a in range(3):
            for bc in range(9):
                weight = prod_v[9 * a + bc, :, x]
                for j in range(3):
                    totals[j] = totals[j] + weight * shifted_v[j, bc, x + a][None]
        for j in range(3):
            drag_v[j, :, x] = src_v[1, :, x] * totals[j] - occ_v[:, x] * src_v[2 + j, :, x]
        return carry

    lax.fori_loop(0, 4, drag, 0)
    drag_out = pltpu.make_async_copy(drag_v, drag_h, out_sem.at[0])
    drag_out.start()

    def finish(k, carry):
        for n in range(2):
            s = (-1, 1)[n]
            wait_recv((s, 0, 0), fx_v.at[n, k], rx_v.at[n, k], x_ss.at[n, k], x_rs.at[n, k])
            wait_recv((2 * s, 0, 0), fx2_v.at[n, k], rx2_v.at[n, k], x2_ss.at[n, k], x2_rs.at[n, k])
        total = out_v[k] + (rx_v[0, k] + rx_v[1, k])
        out_v[k] = jnp.concatenate([total[0:1] + rx2_v[0, k][None], total[1:3], total[3:4] + rx2_v[1, k][None]], axis=0)
        return carry

    lax.fori_loop(0, 5, finish, 0)
    filtered_out = pltpu.make_async_copy(out_v, filtered_h, out_sem.at[1])
    filtered_out.start()

    def sent(k, carry):
        for n in range(2):
            wait_send(*y_copy(n, k))
        for item in x_copies(k):
            wait_send(*item)
        return carry

    lax.fori_loop(0, 5, sent, 0)
    for item in gas_x + z_copies + d_copies + gy_copies + gz_copies + gd_copies:
        wait_send(*item)
    drag_out.wait()
    filtered_out.wait()


def solution(mesh):
    sizes = tuple(mesh.shape[name] for name in ("gx", "gy", "gz"))
    dma = pltpu.SemaphoreType.DMA

    def vmem(*shape):
        return pltpu.VMEM(shape + (8, 128), F32)

    def shards(counts, offsets, volume, beta, particle_velocity, gas_velocity):
        any_space = pl.BlockSpec(memory_space=pl.ANY)
        return pl.pallas_call(
            functools.partial(kernel, sizes),
            out_shape=(jax.ShapeDtypeStruct((5, 4, 8, 128), F32), jax.ShapeDtypeStruct((3, 4, 4, 8, 128), F32)),
            in_specs=[any_space] * 6,
            out_specs=(any_space, any_space),
            scratch_shapes=[
                pltpu.VMEM((4, 8, 128), jnp.int32), vmem(3, 4, 4), vmem(5, 4, 4), vmem(3, 4, 4), vmem(3, 6),
                vmem(4, 4), vmem(27, 4, 4), vmem(3, 9, 6),
                vmem(5, 6), vmem(5, 6), vmem(5), vmem(5),
                vmem(2, 5, 7), vmem(2, 5, 2), vmem(4, 5), vmem(2, 5, 7), vmem(2, 5, 2), vmem(4, 5),
                vmem(2, 3), vmem(3), vmem(2, 3), vmem(2, 3), vmem(4, 3),
                vmem(2, 5, 4), vmem(2, 5), vmem(2, 5, 4), vmem(2, 5), vmem(5, 4), vmem(3, 4, 4),
                dma((6,)), dma((2,)), dma((2, 5)), dma((2, 5)), dma((2,)), dma((2,)), dma((4,)), dma((4,)),
                dma((2,)), dma((2,)), dma((2,)), dma((2,)), dma((2,)), dma((2,)), dma((4,)), dma((4,)),
                dma((2, 5)), dma((2, 5)), dma((2, 5)), dma((2, 5)),
            ],
            compiler_params=pltpu.CompilerParams(
                collective_id=0, has_side_effects=True, vmem_limit_bytes=32 * 2**20),
            name="deposit_filter_drag",
        )(*[pltpu.with_memory_space_constraint(v, pltpu.HBM) for v in (
            counts, offsets, volume, beta, particle_velocity, gas_velocity)])

    in_specs = (
        P("gx", "gy", "gz"),
        P(None, None, "gx", "gy", "gz"),
        P(None, "gx", "gy", "gz"),
        P(None, "gx", "gy", "gz"),
        P(None, None, "gx", "gy", "gz"),
        P(None, "gx", "gy", "gz"),
    )
    out_specs = (P(None, "gx", "gy", "gz"), P(None, None, "gx", "gy", "gz"))
    return jax.shard_map(shards, mesh=mesh, in_specs=in_specs, out_specs=out_specs, check_vma=False)
```

```python
import functools
import math

import jax
import jax.numpy as jnp
import numpy as np
from jax import lax
from jax.experimental import pallas as pl
from jax.experimental.pallas import tpu as pltpu
from jax.sharding import PartitionSpec as P

MESH = pl.DeviceIdType.MESH
F32 = jnp.float32
SIGMA = 0.6
INV_S2 = 1.0 / (SIGMA * SIGMA)
CENTRE = math.exp(0.5 * INV_S2)
ITERS = 4
FILTER = 2.0

GROUPS = ((0, 2), (2, 4), (4, 5))
DIAG = ((-1, -1), (-1, 1), (1, -1), (1, 1))
ALL = ([(0, a, b) for a in (-1, 0, 1) for b in (-1, 0, 1) if (a, b) != (0, 0)]
       + [(-1, 0, 0), (1, 0, 0), (-2, 0, 0), (2, 0, 0)])


def filter_taps():
    unit = np.zeros((2 * ITERS + 3,) * 3)
    unit[(ITERS + 1,) * 3] = 1.0
    current = unit
    for _ in range(ITERS):
        around = sum(np.roll(current, step, axis) for axis in range(3) for step in (-1, 1))
        current = (unit + FILTER * around) / (1.0 + 6.0 * FILTER)
    return current[ITERS + 1:, ITERS + 1:, ITERS + 1:]


TAPS = filter_taps()


def rot(value, shift, axis):
    size = value.shape[axis]
    return pltpu.roll(value, shift % size, axis)


def kernel(sizes, counts_h, offsets_h, volume_h, beta_h, pv_h, gas_h, filtered_o, drag_o,
           counts_v, offsets_v, src_v, pv_v, gas_v, occ_v, prod_v, shifted_v, dm_v, dy_v, dz_v, dyz_v,
           sy_v, sz_v, sd_v, sx_v, sx2_v, ry_v, rz_v, rd_v, rx_v, rx2_v, sgz_v,
           in_sem, y_ss, z_ss, d_ss, x_ss, x2_ss, y_rs, z_rs, d_rs, gx_rs, x_rs, x2_rs, late_sem):
    me = (lax.axis_index("gx"), lax.axis_index("gy"), lax.axis_index("gz"))

    def near(step):
        place = tuple(me[i] + step[i] for i in range(3))
        ok = None
        for i in range(3):
            if step[i]:
                inside = place[i] >= 0 if step[i] < 0 else place[i] < sizes[i]
                ok = inside if ok is None else ok & inside
        origin = None
        if max(step) <= 0:
            origin = (place[0] == 0) & (place[1] == 0) & (place[2] == 0)
        return place, ok, origin

    def copy(step, src, dst, ssem, rsem):
        return pltpu.make_async_remote_copy(src_ref=src, dst_ref=dst, send_sem=ssem, recv_sem=rsem,
                                            device_id=near(step)[0], device_id_type=MESH)

    def send(items, to_origin=None):
        _, ok, origin = near(items[0][0])
        if to_origin is not None and origin is not None:
            ok = origin if to_origin else ok & jnp.logical_not(origin)
        elif to_origin:
            return

        @pl.when(ok)
        def _():
            for item in items:
                copy(*item).start()

    def wait_recv(step, dst, rsem):
        @pl.when(near(step)[1])
        def _():
            copy(step, dst, dst, rsem, rsem).wait_recv()

    def wait_send(step, src, ssem):
        @pl.when(near(step)[1])
        def _():
            copy(step, src, src, ssem, ssem).wait_send()

    loads = [
        pltpu.make_async_copy(offsets_h, offsets_v, in_sem.at[0]),
        pltpu.make_async_copy(counts_h, counts_v, in_sem.at[1]),
        pltpu.make_async_copy(gas_h, gas_v.at[:, pl.ds(1, 4)], in_sem.at[2]),
        pltpu.make_async_copy(volume_h, src_v.at[0], in_sem.at[3]),
        pltpu.make_async_copy(beta_h, src_v.at[1], in_sem.at[4]),
        pltpu.make_async_copy(pv_h, pv_v, in_sem.at[5]),
    ]
    for load in loads:
        load.start()

    is_origin = (me[0] == 0) & (me[1] == 0) & (me[2] == 0)
    barrier = pltpu.get_barrier_semaphore()
    greeted = jnp.int32(0)
    for step in ALL:
        place, ok, origin = near(step)
        greets = ok if origin is None else ok & jnp.logical_not(origin)
        greeted = greeted + greets.astype(jnp.int32)

        @pl.when(ok & jnp.logical_not(is_origin))
        def _():
            pl.semaphore_signal(barrier, inc=1, device_id=place, device_id_type=MESH)

    @pl.when(is_origin)
    def _():
        pl.semaphore_wait(barrier, greeted)
        for step in ALL:
            if min(step) >= 0:
                place, ok, _ = near(step)

                @pl.when(ok)
                def _():
                    pl.semaphore_signal(late_sem, inc=1, device_id=place, device_id_type=MESH)

    def clear(step, refs):
        @pl.when(jnp.logical_not(near(step)[1]))
        def _():
            for ref in refs:
                ref[...] = jnp.zeros(ref.shape, F32)

    for n, s in enumerate((-1, 1)):
        clear((s, 0, 0), [rx_v.at[n]])
        clear((2 * s, 0, 0), [rx2_v.at[n]])
        clear((0, s, 0), [ry_v.at[n]])
        clear((0, 0, s), [rz_v.at[n]])
    for n, (a, b) in enumerate(DIAG):
        clear((0, a, b), [rd_v.at[n]])

    row = lax.broadcasted_iota(jnp.int32, (8, 128), 0)
    lane = lax.broadcasted_iota(jnp.int32, (8, 128), 1)
    slot, col = lane >> 3, lane & 7
    row0, row7, row_low = row == 0, row == 7, row < 4
    lane0, lane127, col_low = lane == 0, lane == 127, col < 4

    edge_rows = (row_low & (me[1] == sizes[1] - 1)) | (~row_low & (me[1] == 0))
    edge_cols = (col_low & (me[2] == 0)) | (~col_low & (me[2] == sizes[2] - 1))
    keep_first, keep_last = (me[0] > 0).astype(F32), (me[0] < sizes[0] - 1).astype(F32)

    def mirror_rows(tiles, spill):
        image = jnp.where((row == 1) | (row == 4), rot(tiles, 2, tiles.ndim - 2), jnp.where(
            (row == 2) | (row == 5), rot(tiles, 4, tiles.ndim - 2),
            jnp.where((row == 3) | (row == 6), rot(tiles, 6, tiles.ndim - 2), 0.0)))
        return jnp.where(edge_rows, -image, spill)

    def mirror_cols(packed, spill):
        image = jnp.where(col == 0, rot(packed, -6, 1), jnp.where(col == 1, rot(packed, -4, 1), jnp.where(
            col == 2, rot(packed, -2, 1), jnp.where(col == 5, rot(packed, 2, 1), jnp.where(
                col == 6, rot(packed, 4, 1), jnp.where(col == 7, rot(packed, 6, 1), 0.0))))))
        return jnp.where(edge_cols, -image, spill)

    def part(n, ref, per, g):
        first, last = GROUPS[g]
        return ref.at[n, pl.ds(per * first, per * (last - first))]

    def gas_x(n):
        return ((-1, 1)[n], 0, 0), sx_v.at[n, pl.ds(20, 3)], rx_v.at[1 - n, pl.ds(20, 3)], x_ss.at[n], gx_rs.at[1 - n]

    def send_gas_x(to_origin):
        for n in range(2):
            send([gas_x(n)], to_origin)

    def send_group(g, to_origin):
        for n, (a, b) in enumerate(DIAG):
            send([((0, a, b), part(n, sd_v, 1, g), part(3 - n, rd_v, 1, g), d_ss.at[n], d_rs.at[3 - n, g])], to_origin)
        for n in range(2):
            send([((0, 0, (-1, 1)[n]), part(n, sz_v, 2, g), part(1 - n, rz_v, 2, g), z_ss.at[n], z_rs.at[1 - n, g])],
                 to_origin)
            send([((0, (-1, 1)[n], 0), part(n, sy_v, 7, g), part(1 - n, ry_v, 7, g), y_ss.at[n], y_rs.at[1 - n, g])],
                 to_origin)

    def wait_group(g):
        for n in range(2):
            wait_recv((0, (-1, 1)[n], 0), part(n, ry_v, 7, g), y_rs.at[n, g])
            wait_recv((0, 0, (-1, 1)[n]), part(n, rz_v, 2, g), z_rs.at[n, g])
        for n, (a, b) in enumerate(DIAG):
            wait_recv((0, a, b), part(n, rd_v, 1, g), d_rs.at[n, g])

    loads[0].wait()
    loads[1].wait()

    def products(s, carry):
        occ = jnp.where(counts_v[...] > s, F32(1.0), F32(0.0))
        occ_v[s] = occ
        weights, norm = [], None
        for axis in range(3):
            t = jnp.exp((0.5 - offsets_v[axis, s]) * INV_S2)
            low, mid = t * t, CENTRE * t
            total = low + mid + 1.0
            norm = total if norm is None else norm * total
            weights.append((low, mid))
        scale = occ / norm
        wx = (weights[0][0] * scale, weights[0][1] * scale, scale)
        for a in range(3):
            for b in range(3):
                xy = wx[a] * weights[1][b] if b < 2 else wx[a]
                for c in range(3):
                    prod_v[9 * a + 3 * b + c, s] = xy * weights[2][c] if c < 2 else xy
        return carry

    lax.fori_loop(0, 4, products, 0, unroll=True)
    loads[2].wait()
    for j in range(3):
        sx_v[0, 20 + j] = gas_v[j, 1]
        sx_v[1, 20 + j] = gas_v[j, 4]

    @pl.when(is_origin)
    def _():
        send_gas_x(None)

    for load in loads[3:]:
        load.wait()
    for j in range(3):
        src_v[2 + j] = src_v[1] * pv_v[j]

    def pack(planes, first):
        result = jnp.zeros((8, 128), F32)
        for i in range(planes.shape[0]):
            result = jnp.where(slot == first + i, rot(planes[i], 8 * (first + i) + 4, 1), result)
        return result

    def unpack(tile, first, count):
        return jnp.stack([rot(tile, -(8 * (first + i) + 4), 1) for i in range(count)])

    def deposit(k, carry):
        src = [src_v[k, s] for s in range(4)]
        by_z = []
        for c in range(3):
            by_y = []
            for b in range(3):
                by_x = []
                for a in range(3):
                    total = src[0] * prod_v[9 * a + 3 * b + c, 0]
                    for s in range(1, 4):
                        total = total + src[s] * prod_v[9 * a + 3 * b + c, s]
                    by_x.append(total)
                lo, mid, hi = by_x
                by_y.append(jnp.concatenate([
                    lo[0:1], lo[1:2] + mid[0:1], lo[2:4] + mid[1:3] + hi[0:2], mid[3:4] + hi[2:3], hi[3:4]], axis=0))
            up, down = rot(by_y[2], 1, 1), rot(by_y[0], -1, 1)
            by_z.append((by_y[1] + jnp.where(row0, 0.0, up) + jnp.where(row7, 0.0, down),
                         jnp.where(row0, up, jnp.where(row7, down, 0.0))))
        main, packs = [], []
        for kind in range(2):
            up, down = rot(by_z[2][kind], 1, 2), rot(by_z[0][kind], -1, 2)
            spill = jnp.where(lane0, up, jnp.where(lane127, down, 0.0))
            main.append(by_z[1][kind] + jnp.where(lane0, 0.0, up) + jnp.where(lane127, 0.0, down))
            packed = rot(spill[0], 36, 1) * keep_first
            for i in range(1, 5):
                packed = packed + rot(spill[i], 8 * i + 36, 1)
            packs.append(packed + rot(spill[5], 76, 1) * keep_last)
        m, y = [jnp.concatenate([v[0:1] * keep_first, v[1:5], v[5:6] * keep_last], axis=0) for v in main]
        z, yz = packs
        y, yz = mirror_rows(m, y), mirror_rows(z, yz)
        mp, yp = pack(m, 4), pack(y, 4)
        z, yz = mirror_cols(mp, z), mirror_cols(yp, yz)
        dm_v[k], dy_v[k], dz_v[k], dyz_v[k] = m, y, z, yz
        sy_v[0, pl.ds(7 * k, 6)] = jnp.where(row_low, m, y)
        sy_v[1, pl.ds(7 * k, 6)] = jnp.where(row_low, y, m)
        sy_v[0, 7 * k + 6] = jnp.where(row_low, z, yz)
        sy_v[1, 7 * k + 6] = jnp.where(row_low, yz, z)
        zm = (jnp.where(col_low, z, mp), jnp.where(col_low, mp, z))
        zy = (jnp.where(col_low, yz, yp), jnp.where(col_low, yp, yz))
        for n in range(2):
            sz_v[n, 2 * k], sz_v[n, 2 * k + 1] = zm[n], zy[n]
        for n, (a, b) in enumerate(DIAG):
            first, second = (zm, zy) if a < 0 else (zy, zm)
            sd_v[n, k] = jnp.where(row_low, first[(b + 1) // 2], second[(b + 1) // 2])
        return carry

    for g in range(3):
        lax.fori_loop(*GROUPS[g], deposit, 0, unroll=True)

        @pl.when(is_origin)
        def _():
            send_group(g, None)

    @pl.when(jnp.logical_not(is_origin))
    def _():
        pl.semaphore_wait(barrier, greeted)
        send_gas_x(False)
        for g in range(3):
            send_group(g, False)

    by_origin = jnp.bool_(False)
    for step in ALL:
        if max(step) <= 0:
            by_origin = by_origin | near(step)[2]

    @pl.when(by_origin)
    def _():
        pl.semaphore_wait(late_sem, 1)
        send_gas_x(True)
        for g in range(3):
            send_group(g, True)

    for n in range(2):
        wait_recv(((-1, 1)[n], 0, 0), rx_v.at[n, pl.ds(20, 3)], gx_rs.at[n])
    for j in range(3):
        gas_v[j, 0] = rx_v[0, 20 + j]
        gas_v[j, 5] = rx_v[1, 20 + j]
        sgz_v[j] = pack(gas_v[j], 4)
        for i in range(6):
            sy_v[0, 35 + j, pl.ds(i, 1), :] = gas_v[j, i, pl.ds(0, 1), :]
            sy_v[1, 35 + j, pl.ds(i, 1), :] = gas_v[j, i, pl.ds(7, 1), :]
        for n in range(2):
            sy_v[n, 35 + j, pl.ds(6, 2), :] = jnp.zeros((2, 128), F32)
    for n in range(2):
        send([((0, (-1, 1)[n], 0), sy_v.at[n, pl.ds(35, 3)], ry_v.at[1 - n, pl.ds(35, 3)], y_ss.at[n], y_rs.at[1 - n, 3])])
        send([((0, 0, (-1, 1)[n]), sgz_v, rz_v.at[1 - n, pl.ds(10, 3)], z_ss.at[n], z_rs.at[1 - n, 3])])
    for n, (a, b) in enumerate(DIAG):
        send([((0, a, b), sgz_v, rd_v.at[3 - n, pl.ds(5, 3)], d_ss.at[n], d_rs.at[3 - n, 3])])

    def filter_one(k, carry):
        below, above = ry_v[0, pl.ds(7 * k, 6)], ry_v[1, pl.ds(7 * k, 6)]
        below_z, above_z = ry_v[0, 7 * k + 6], ry_v[1, 7 * k + 6]
        m = dm_v[k] + jnp.where(row_low[None], below, above)
        y = dy_v[k] + jnp.where(row_low[None], above, below)
        side = []
        for n, b in enumerate((0, 1)):
            lower, upper = rd_v[b, k], rd_v[2 + b, k]
            side.append((rz_v[n, 2 * k] + jnp.where(row_low, lower, upper),
                         rz_v[n, 2 * k + 1] + jnp.where(row_low, upper, lower)))
        z = dz_v[k] + jnp.where(col_low, side[0][0], side[1][0]) + jnp.where(row_low, below_z, above_z)
        yz = dyz_v[k] + jnp.where(col_low, side[0][1], side[1][1]) + jnp.where(row_low, above_z, below_z)
        ends = (lane0 | lane127)[None]
        m = m + jnp.where(ends, unpack(jnp.where(col_low, side[1][0], side[0][0]), 4, 6), 0.0)
        y = y + jnp.where(ends, unpack(jnp.where(col_low, side[1][1], side[0][1]), 4, 6), 0.0)
        edge_m, edge_y = unpack(z, 4, 6), unpack(yz, 4, 6)
        pushed = [None] * 14
        for i in range(6):
            parts = [None] * 5

            def add(sum_s, sum_c, value):
                for d in range(5 - sum_s - sum_c):
                    term = value * F32(TAPS[d, sum_s, sum_c])
                    parts[d] = term if parts[d] is None else parts[d] + term

            for c in range(5):
                rows = []
                for kind, (tile, edge) in enumerate(((m[i], edge_m[i]), (y[i], edge_y[i]))):
                    if c and not (kind and c == 4):
                        tile = (rot(jnp.where(lane < c, edge, tile), -c, 1)
                                + rot(jnp.where(lane >= 128 - c, edge, tile), c, 1))
                    rows.append(tile)
                add(0, c, rows[0])
                for s in range(1, 5 - c):
                    add(s, c, rot(jnp.where(row < s, rows[1], rows[0]), -s, 0)
                        + rot(jnp.where(row >= 8 - s, rows[1], rows[0]), s, 0))
            for d in range(5):
                for q in {i + 4 - d, i + 4 + d}:
                    pushed[q] = parts[d] if pushed[q] is None else pushed[q] + parts[d]
        for i in range(4):
            sx_v[0, 4 * k + i] = pushed[1 + i]
            filtered_o[k, i] = pushed[5 + i]
            sx_v[1, 4 * k + i] = pushed[9 + i]
        sx2_v[0, k] = pushed[0]
        sx2_v[1, k] = pushed[13]

        @pl.when(me[0] == 0)
        def _():
            for i in range(3):
                rx_v[0, 4 * k + i] = -pushed[3 - i]

        @pl.when(me[0] == sizes[0] - 1)
        def _():
            for i in range(1, 4):
                rx_v[1, 4 * k + i] = -pushed[13 - i]
        return carry

    for g in range(3):
        wait_group(g)
        lax.fori_loop(*GROUPS[g], filter_one, 0, unroll=True)
        for n, s in enumerate((-1, 1)):
            send([((s, 0, 0), part(n, sx_v, 4, g), part(1 - n, rx_v, 4, g), x_ss.at[n], x_rs.at[1 - n])])
            send([((2 * s, 0, 0), part(n, sx2_v, 1, g), part(1 - n, rx2_v, 1, g), x2_ss.at[n], x2_rs.at[1 - n])])

    for n in range(2):
        wait_recv((0, (-1, 1)[n], 0), ry_v.at[n, pl.ds(35, 3)], y_rs.at[n, 3])
        wait_recv((0, 0, (-1, 1)[n]), rz_v.at[n, pl.ds(10, 3)], z_rs.at[n, 3])
    for n, (a, b) in enumerate(DIAG):
        wait_recv((0, a, b), rd_v.at[n, pl.ds(5, 3)], d_rs.at[n, 3])

    def shift(j, carry):
        tiles = gas_v[j]
        below, above = ry_v[0, 35 + j], ry_v[1, 35 + j]
        rows = jnp.stack([jnp.where(row0, jnp.broadcast_to(above[i:i + 1], (8, 128)),
                                    jnp.broadcast_to(below[i:i + 1], (8, 128))) for i in range(6)])
        halo_m = jnp.where(col_low, rz_v[0, 10 + j], rz_v[1, 10 + j])
        halo_y = jnp.where(col_low, jnp.where(row0, rd_v[2, 5 + j], rd_v[0, 5 + j]),
                           jnp.where(row0, rd_v[3, 5 + j], rd_v[1, 5 + j]))
        variants = []
        for value, halo in ((tiles, halo_m), (rows, halo_y)):
            edge = unpack(halo, 4, 6)
            variants.append((rot(jnp.where(lane127[None], edge, value), 1, 2), value,
                             rot(jnp.where(lane0[None], edge, value), -1, 2)))
        for c in range(3):
            value, halo = variants[0][c], variants[1][c]
            shifted_v[j, c] = rot(jnp.where(row7[None], halo, value), 1, 1)
            shifted_v[j, 3 + c] = value
            shifted_v[j, 6 + c] = rot(jnp.where(row0[None], halo, value), -1, 1)
        return carry

    lax.fori_loop(0, 3, shift, 0, unroll=True)

    def drag(x, carry):
        totals = [jnp.zeros((4, 8, 128), F32) for _ in range(3)]
        for a in range(3):
            for bc in range(9):
                weight = prod_v[9 * a + bc, :, x]
                for j in range(3):
                    totals[j] = totals[j] + weight * shifted_v[j, bc, x + a][None]
        for j in range(3):
            drag_o[j, :, x] = src_v[1, :, x] * totals[j] - occ_v[:, x] * src_v[2 + j, :, x]
        return carry

    lax.fori_loop(0, 4, drag, 0, unroll=True)

    for n, s in enumerate((-1, 1)):
        wait_recv((s, 0, 0), rx_v.at[n, pl.ds(0, 20)], x_rs.at[n])
        wait_recv((2 * s, 0, 0), rx2_v.at[n], x2_rs.at[n])
    for k in range(5):
        for i in range(4):
            total = filtered_o[k, i] + (rx_v[0, 4 * k + i] + rx_v[1, 4 * k + i])
            if i in (0, 3):
                total = total + rx2_v[i // 3, k]
            filtered_o[k, i] = total

    for n, s in enumerate((-1, 1)):
        wait_send((0, s, 0), sy_v.at[n], y_ss.at[n])
        wait_send((0, 0, s), sz_v.at[n], z_ss.at[n])
        wait_send((s, 0, 0), sx_v.at[n], x_ss.at[n])
        wait_send((2 * s, 0, 0), sx2_v.at[n], x2_ss.at[n])
    for n, (a, b) in enumerate(DIAG):
        wait_send((0, a, b), sd_v.at[n], d_ss.at[n])


def store(filtered_v, drag_v, filtered_h, drag_h, sem):
    copies = [pltpu.make_async_copy(filtered_v, filtered_h, sem.at[0]), pltpu.make_async_copy(drag_v, drag_h, sem.at[1])]
    for item in copies:
        item.start()
    for item in copies:
        item.wait()


def solution(mesh):
    sizes = tuple(mesh.shape[name] for name in ("gx", "gy", "gz"))
    dma = pltpu.SemaphoreType.DMA

    def vmem(*shape):
        return pltpu.VMEM(shape + (8, 128), F32)

    def shards(counts, offsets, volume, beta, particle_velocity, gas_velocity):
        any_space = pl.BlockSpec(memory_space=pl.ANY)
        out_shape = (jax.ShapeDtypeStruct((5, 4, 8, 128), F32), jax.ShapeDtypeStruct((3, 4, 4, 8, 128), F32))
        filtered, drag = pl.pallas_call(
            functools.partial(kernel, sizes),
            out_shape=out_shape,
            in_specs=[any_space] * 6,
            out_specs=(pl.BlockSpec(memory_space=pltpu.VMEM),) * 2,
            scratch_shapes=[
                pltpu.VMEM((4, 8, 128), jnp.int32), vmem(3, 4, 4), vmem(5, 4, 4), vmem(3, 4, 4), vmem(3, 6),
                vmem(4, 4), vmem(27, 4, 4), vmem(3, 9, 6), vmem(5, 6), vmem(5, 6), vmem(5), vmem(5),
                vmem(2, 38), vmem(2, 13), vmem(4, 8), vmem(2, 23), vmem(2, 5),
                vmem(2, 38), vmem(2, 13), vmem(4, 8), vmem(2, 23), vmem(2, 5), vmem(3),
                dma((6,)), dma((2,)), dma((2,)), dma((4,)), dma((2,)), dma((2,)),
                dma((2, 4)), dma((2, 4)), dma((4, 4)), dma((2,)), dma((2,)), dma((2,)), pltpu.SemaphoreType.REGULAR,
            ],
            compiler_params=pltpu.CompilerParams(
                collective_id=0, has_side_effects=True, vmem_limit_bytes=32 * 2**20),
            name="deposit_filter_drag",
        )(*[pltpu.with_memory_space_constraint(v, pltpu.HBM) for v in (
            counts, offsets, volume, beta, particle_velocity, gas_velocity)])
        return pl.pallas_call(
            store, out_shape=out_shape, in_specs=[any_space] * 2, out_specs=(any_space,) * 2,
            scratch_shapes=[dma((2,))], compiler_params=pltpu.CompilerParams(vmem_limit_bytes=2**20), name="store",
        )(filtered, drag)

    in_specs = (
        P("gx", "gy", "gz"),
        P(None, None, "gx", "gy", "gz"),
        P(None, "gx", "gy", "gz"),
        P(None, "gx", "gy", "gz"),
        P(None, None, "gx", "gy", "gz"),
        P(None, "gx", "gy", "gz"),
    )
    out_specs = (P(None, "gx", "gy", "gz"), P(None, None, "gx", "gy", "gz"))
    return jax.shard_map(shards, mesh=mesh, in_specs=in_specs, out_specs=out_specs, check_vma=False)
```

```python
import functools
import math

import jax
import jax.numpy as jnp
import numpy as np
from jax import lax
from jax.experimental import pallas as pl
from jax.experimental.pallas import tpu as pltpu
from jax.sharding import PartitionSpec as P

MESH = pl.DeviceIdType.MESH
F32 = jnp.float32
SIGMA = 0.6
INV_S2 = 1.0 / (SIGMA * SIGMA)
CENTRE = math.exp(0.5 * INV_S2)
ITERS = 4
FILTER = 2.0

GROUPS = ((0, 2), (2, 4), (4, 5))
DIAG = ((-1, -1), (-1, 1), (1, -1), (1, 1))
ALL = ([(0, a, b) for a in (-1, 0, 1) for b in (-1, 0, 1) if (a, b) != (0, 0)]
       + [(-1, 0, 0), (1, 0, 0), (-2, 0, 0), (2, 0, 0)])


def filter_taps():
    unit = np.zeros((2 * ITERS + 3,) * 3)
    unit[(ITERS + 1,) * 3] = 1.0
    current = unit
    for _ in range(ITERS):
        around = sum(np.roll(current, step, axis) for axis in range(3) for step in (-1, 1))
        current = (unit + FILTER * around) / (1.0 + 6.0 * FILTER)
    return current[ITERS + 1:, ITERS + 1:, ITERS + 1:]


TAPS = filter_taps()


def rot(value, shift, axis):
    size = value.shape[axis]
    return pltpu.roll(value, shift % size, axis)


def kernel(sizes, counts_h, offsets_h, volume_h, beta_h, pv_h, gas_h, filtered_o, drag_o,
           counts_v, offsets_v, src_v, pv_v, gas_v, occ_v, prod_v, shifted_v, dm_v, dy_v, dz_v, dyz_v,
           sy_v, sz_v, sd_v, sx_v, sx2_v, ry_v, rz_v, rd_v, rx_v, rx2_v, sgz_v,
           in_sem, y_ss, z_ss, d_ss, x_ss, x2_ss, y_rs, z_rs, d_rs, gx_rs, x_rs, x2_rs, late_sem):
    me = (lax.axis_index("gx"), lax.axis_index("gy"), lax.axis_index("gz"))

    def near(step):
        place = tuple(me[i] + step[i] for i in range(3))
        ok = None
        for i in range(3):
            if step[i]:
                inside = place[i] >= 0 if step[i] < 0 else place[i] < sizes[i]
                ok = inside if ok is None else ok & inside
        origin = None
        if max(step) <= 0:
            origin = (place[0] == 0) & (place[1] == 0) & (place[2] == 0)
        return place, ok, origin

    def copy(step, src, dst, ssem, rsem):
        return pltpu.make_async_remote_copy(src_ref=src, dst_ref=dst, send_sem=ssem, recv_sem=rsem,
                                            device_id=near(step)[0], device_id_type=MESH)

    def send(items, to_origin=None):
        _, ok, origin = near(items[0][0])
        if to_origin is not None and origin is not None:
            ok = origin if to_origin else ok & jnp.logical_not(origin)
        elif to_origin:
            return

        @pl.when(ok)
        def _():
            for item in items:
                copy(*item).start()

    def wait_recv(step, dst, rsem):
        @pl.when(near(step)[1])
        def _():
            copy(step, dst, dst, rsem, rsem).wait_recv()

    def wait_send(step, src, ssem):
        @pl.when(near(step)[1])
        def _():
            copy(step, src, src, ssem, ssem).wait_send()

    is_origin = (me[0] == 0) & (me[1] == 0) & (me[2] == 0)
    barrier = pltpu.get_barrier_semaphore()
    late = [step for step in ALL if min(step) >= 0 and all(s < n for s, n in zip(step, sizes))]

    @pl.when(is_origin)
    def _():
        pl.semaphore_wait(barrier, len(late))
        for step in late:
            pl.semaphore_signal(late_sem, inc=1, device_id=step, device_id_type=MESH)

    loads = [
        pltpu.make_async_copy(offsets_h, offsets_v, in_sem.at[0]),
        pltpu.make_async_copy(counts_h, counts_v, in_sem.at[1]),
        pltpu.make_async_copy(gas_h, gas_v.at[:, pl.ds(1, 4)], in_sem.at[2]),
        pltpu.make_async_copy(volume_h, src_v.at[0], in_sem.at[3]),
        pltpu.make_async_copy(beta_h, src_v.at[1], in_sem.at[4]),
        pltpu.make_async_copy(pv_h, pv_v, in_sem.at[5]),
    ]
    for load in loads:
        load.start()

    greeted = jnp.int32(0)
    for step in ALL:
        _, ok, origin = near(step)
        greets = ok if origin is None else ok & jnp.logical_not(origin)
        greeted = greeted + greets.astype(jnp.int32)

    @pl.when(jnp.logical_not(is_origin))
    def _():
        for step in ALL:
            place, ok, _ = near(step)

            @pl.when(ok)
            def _():
                pl.semaphore_signal(barrier, inc=1, device_id=place, device_id_type=MESH)

    def clear(step, refs):
        @pl.when(jnp.logical_not(near(step)[1]))
        def _():
            for ref in refs:
                ref[...] = jnp.zeros(ref.shape, F32)

    for n, s in enumerate((-1, 1)):
        clear((s, 0, 0), [rx_v.at[n]])
        clear((2 * s, 0, 0), [rx2_v.at[n]])
        clear((0, s, 0), [ry_v.at[n]])
        clear((0, 0, s), [rz_v.at[n]])
    for n, (a, b) in enumerate(DIAG):
        clear((0, a, b), [rd_v.at[n]])

    row = lax.broadcasted_iota(jnp.int32, (8, 128), 0)
    lane = lax.broadcasted_iota(jnp.int32, (8, 128), 1)
    slot, col = lane >> 3, lane & 7
    row0, row7, row_low = row == 0, row == 7, row < 4
    lane0, lane127, col_low = lane == 0, lane == 127, col < 4

    edge_rows = (row_low & (me[1] == sizes[1] - 1)) | (~row_low & (me[1] == 0))
    edge_cols = (col_low & (me[2] == 0)) | (~col_low & (me[2] == sizes[2] - 1))
    keep_first, keep_last = (me[0] > 0).astype(F32), (me[0] < sizes[0] - 1).astype(F32)

    def mirror_rows(tiles, spill):
        image = jnp.where((row == 1) | (row == 4), rot(tiles, 2, tiles.ndim - 2), jnp.where(
            (row == 2) | (row == 5), rot(tiles, 4, tiles.ndim - 2),
            jnp.where((row == 3) | (row == 6), rot(tiles, 6, tiles.ndim - 2), 0.0)))
        return jnp.where(edge_rows, -image, spill)

    def mirror_cols(packed, spill):
        image = jnp.where(col == 0, rot(packed, -6, 1), jnp.where(col == 1, rot(packed, -4, 1), jnp.where(
            col == 2, rot(packed, -2, 1), jnp.where(col == 5, rot(packed, 2, 1), jnp.where(
                col == 6, rot(packed, 4, 1), jnp.where(col == 7, rot(packed, 6, 1), 0.0))))))
        return jnp.where(edge_cols, -image, spill)

    def part(n, ref, per, g):
        first, last = GROUPS[g]
        return ref.at[n, pl.ds(per * first, per * (last - first))]

    def gas_x(n):
        return ((-1, 1)[n], 0, 0), sx_v.at[n, pl.ds(20, 3)], rx_v.at[1 - n, pl.ds(20, 3)], x_ss.at[n], gx_rs.at[1 - n]

    def send_gas_x(to_origin):
        for n in range(2):
            send([gas_x(n)], to_origin)

    def send_group(g, to_origin):
        for n, (a, b) in enumerate(DIAG):
            send([((0, a, b), part(n, sd_v, 1, g), part(3 - n, rd_v, 1, g), d_ss.at[n], d_rs.at[3 - n, g])], to_origin)
        for n in range(2):
            send([((0, 0, (-1, 1)[n]), part(n, sz_v, 2, g), part(1 - n, rz_v, 2, g), z_ss.at[n], z_rs.at[1 - n, g])],
                 to_origin)
            send([((0, (-1, 1)[n], 0), part(n, sy_v, 7, g), part(1 - n, ry_v, 7, g), y_ss.at[n], y_rs.at[1 - n, g])],
                 to_origin)

    def wait_group(g):
        for n in range(2):
            wait_recv((0, (-1, 1)[n], 0), part(n, ry_v, 7, g), y_rs.at[n, g])
            wait_recv((0, 0, (-1, 1)[n]), part(n, rz_v, 2, g), z_rs.at[n, g])
        for n, (a, b) in enumerate(DIAG):
            wait_recv((0, a, b), part(n, rd_v, 1, g), d_rs.at[n, g])

    loads[0].wait()
    loads[1].wait()

    def products(s, carry):
        occ = jnp.where(counts_v[...] > s, F32(1.0), F32(0.0))
        occ_v[s] = occ
        weights, norm = [], None
        for axis in range(3):
            t = jnp.exp((0.5 - offsets_v[axis, s]) * INV_S2)
            low, mid = t * t, CENTRE * t
            total = low + mid + 1.0
            norm = total if norm is None else norm * total
            weights.append((low, mid))
        scale = occ / norm
        wx = (weights[0][0] * scale, weights[0][1] * scale, scale)
        for a in range(3):
            for b in range(3):
                xy = wx[a] * weights[1][b] if b < 2 else wx[a]
                for c in range(3):
                    prod_v[9 * a + 3 * b + c, s] = xy * weights[2][c] if c < 2 else xy
        return carry

    lax.fori_loop(0, 4, products, 0, unroll=True)
    loads[2].wait()
    for j in range(3):
        sx_v[0, 20 + j] = gas_v[j, 1]
        sx_v[1, 20 + j] = gas_v[j, 4]

    @pl.when(is_origin)
    def _():
        send_gas_x(None)

    for load in loads[3:]:
        load.wait()
    for j in range(3):
        src_v[2 + j] = src_v[1] * pv_v[j]

    def pack(planes, first):
        result = jnp.zeros((8, 128), F32)
        for i in range(planes.shape[0]):
            result = jnp.where(slot == first + i, rot(planes[i], 8 * (first + i) + 4, 1), result)
        return result

    def unpack(tile, first, count):
        return jnp.stack([rot(tile, -(8 * (first + i) + 4), 1) for i in range(count)])

    def deposit(k, carry):
        src = [src_v[k, s] for s in range(4)]
        by_z = []
        for c in range(3):
            by_y = []
            for b in range(3):
                by_x = []
                for a in range(3):
                    total = src[0] * prod_v[9 * a + 3 * b + c, 0]
                    for s in range(1, 4):
                        total = total + src[s] * prod_v[9 * a + 3 * b + c, s]
                    by_x.append(total)
                lo, mid, hi = by_x
                by_y.append(jnp.concatenate([
                    lo[0:1], lo[1:2] + mid[0:1], lo[2:4] + mid[1:3] + hi[0:2], mid[3:4] + hi[2:3], hi[3:4]], axis=0))
            up, down = rot(by_y[2], 1, 1), rot(by_y[0], -1, 1)
            by_z.append((by_y[1] + jnp.where(row0, 0.0, up) + jnp.where(row7, 0.0, down),
                         jnp.where(row0, up, jnp.where(row7, down, 0.0))))
        main, packs = [], []
        for kind in range(2):
            up, down = rot(by_z[2][kind], 1, 2), rot(by_z[0][kind], -1, 2)
            spill = jnp.where(lane0, up, jnp.where(lane127, down, 0.0))
            main.append(by_z[1][kind] + jnp.where(lane0, 0.0, up) + jnp.where(lane127, 0.0, down))
            packed = rot(spill[0], 36, 1) * keep_first
            for i in range(1, 5):
                packed = packed + rot(spill[i], 8 * i + 36, 1)
            packs.append(packed + rot(spill[5], 76, 1) * keep_last)
        m, y = [jnp.concatenate([v[0:1] * keep_first, v[1:5], v[5:6] * keep_last], axis=0) for v in main]
        z, yz = packs
        y, yz = mirror_rows(m, y), mirror_rows(z, yz)
        mp, yp = pack(m, 4), pack(y, 4)
        z, yz = mirror_cols(mp, z), mirror_cols(yp, yz)
        dm_v[k], dy_v[k], dz_v[k], dyz_v[k] = m, y, z, yz
        sy_v[0, pl.ds(7 * k, 6)] = jnp.where(row_low, m, y)
        sy_v[1, pl.ds(7 * k, 6)] = jnp.where(row_low, y, m)
        sy_v[0, 7 * k + 6] = jnp.where(row_low, z, yz)
        sy_v[1, 7 * k + 6] = jnp.where(row_low, yz, z)
        zm = (jnp.where(col_low, z, mp), jnp.where(col_low, mp, z))
        zy = (jnp.where(col_low, yz, yp), jnp.where(col_low, yp, yz))
        for n in range(2):
            sz_v[n, 2 * k], sz_v[n, 2 * k + 1] = zm[n], zy[n]
        for n, (a, b) in enumerate(DIAG):
            first, second = (zm, zy) if a < 0 else (zy, zm)
            sd_v[n, k] = jnp.where(row_low, first[(b + 1) // 2], second[(b + 1) // 2])
        return carry

    for g in range(3):
        lax.fori_loop(*GROUPS[g], deposit, 0, unroll=True)

        @pl.when(is_origin)
        def _():
            send_group(g, None)

    @pl.when(jnp.logical_not(is_origin))
    def _():
        pl.semaphore_wait(barrier, greeted)
        send_gas_x(False)
        for g in range(3):
            send_group(g, False)

    by_origin = jnp.bool_(False)
    for step in ALL:
        if max(step) <= 0:
            by_origin = by_origin | near(step)[2]

    @pl.when(by_origin)
    def _():
        pl.semaphore_wait(late_sem, 1)
        send_gas_x(True)
        for g in range(3):
            send_group(g, True)

    def spread_gas():
        for n in range(2):
            wait_recv(((-1, 1)[n], 0, 0), rx_v.at[n, pl.ds(20, 3)], gx_rs.at[n])
        for j in range(3):
            gas_v[j, 0] = rx_v[0, 20 + j]
            gas_v[j, 5] = rx_v[1, 20 + j]
            sgz_v[j] = pack(gas_v[j], 4)
            for i in range(6):
                sy_v[0, 35 + j, pl.ds(i, 1), :] = gas_v[j, i, pl.ds(0, 1), :]
                sy_v[1, 35 + j, pl.ds(i, 1), :] = gas_v[j, i, pl.ds(7, 1), :]
            for n in range(2):
                sy_v[n, 35 + j, pl.ds(6, 2), :] = jnp.zeros((2, 128), F32)
        for n in range(2):
            send([((0, (-1, 1)[n], 0), sy_v.at[n, pl.ds(35, 3)], ry_v.at[1 - n, pl.ds(35, 3)], y_ss.at[n], y_rs.at[1 - n, 3])])
            send([((0, 0, (-1, 1)[n]), sgz_v, rz_v.at[1 - n, pl.ds(10, 3)], z_ss.at[n], z_rs.at[1 - n, 3])])
        for n, (a, b) in enumerate(DIAG):
            send([((0, a, b), sgz_v, rd_v.at[3 - n, pl.ds(5, 3)], d_ss.at[n], d_rs.at[3 - n, 3])])

    after_filter = (me[0] == 1) & (me[1] == 0) & (me[2] == 0)
    pl.when(jnp.logical_not(after_filter))(spread_gas)

    def filter_one(k, carry):
        below, above = ry_v[0, pl.ds(7 * k, 6)], ry_v[1, pl.ds(7 * k, 6)]
        below_z, above_z = ry_v[0, 7 * k + 6], ry_v[1, 7 * k + 6]
        m = dm_v[k] + jnp.where(row_low[None], below, above)
        y = dy_v[k] + jnp.where(row_low[None], above, below)
        side = []
        for n, b in enumerate((0, 1)):
            lower, upper = rd_v[b, k], rd_v[2 + b, k]
            side.append((rz_v[n, 2 * k] + jnp.where(row_low, lower, upper),
                         rz_v[n, 2 * k + 1] + jnp.where(row_low, upper, lower)))
        z = dz_v[k] + jnp.where(col_low, side[0][0], side[1][0]) + jnp.where(row_low, below_z, above_z)
        yz = dyz_v[k] + jnp.where(col_low, side[0][1], side[1][1]) + jnp.where(row_low, above_z, below_z)
        ends = (lane0 | lane127)[None]
        m = m + jnp.where(ends, unpack(jnp.where(col_low, side[1][0], side[0][0]), 4, 6), 0.0)
        y = y + jnp.where(ends, unpack(jnp.where(col_low, side[1][1], side[0][1]), 4, 6), 0.0)
        edge_m, edge_y = unpack(z, 4, 6), unpack(yz, 4, 6)
        pushed = [None] * 14
        for i in range(6):
            parts = [None] * 5

            def add(sum_s, sum_c, value):
                for d in range(5 - sum_s - sum_c):
                    term = value * F32(TAPS[d, sum_s, sum_c])
                    parts[d] = term if parts[d] is None else parts[d] + term

            for c in range(5):
                rows = []
                for kind, (tile, edge) in enumerate(((m[i], edge_m[i]), (y[i], edge_y[i]))):
                    if c and not (kind and c == 4):
                        tile = (rot(jnp.where(lane < c, edge, tile), -c, 1)
                                + rot(jnp.where(lane >= 128 - c, edge, tile), c, 1))
                    rows.append(tile)
                add(0, c, rows[0])
                for s in range(1, 5 - c):
                    add(s, c, rot(jnp.where(row < s, rows[1], rows[0]), -s, 0)
                        + rot(jnp.where(row >= 8 - s, rows[1], rows[0]), s, 0))
            for d in range(5):
                for q in {i + 4 - d, i + 4 + d}:
                    pushed[q] = parts[d] if pushed[q] is None else pushed[q] + parts[d]
        for i in range(4):
            sx_v[0, 4 * k + i] = pushed[1 + i]
            filtered_o[k, i] = pushed[5 + i]
            sx_v[1, 4 * k + i] = pushed[9 + i]
        sx2_v[0, k] = pushed[0]
        sx2_v[1, k] = pushed[13]

        @pl.when(me[0] == 0)
        def _():
            for i in range(3):
                rx_v[0, 4 * k + i] = -pushed[3 - i]

        @pl.when(me[0] == sizes[0] - 1)
        def _():
            for i in range(1, 4):
                rx_v[1, 4 * k + i] = -pushed[13 - i]
        return carry

    for g in range(3):
        wait_group(g)
        lax.fori_loop(*GROUPS[g], filter_one, 0, unroll=True)
        for n, s in enumerate((-1, 1)):
            send([((s, 0, 0), part(n, sx_v, 4, g), part(1 - n, rx_v, 4, g), x_ss.at[n], x_rs.at[1 - n])])
            send([((2 * s, 0, 0), part(n, sx2_v, 1, g), part(1 - n, rx2_v, 1, g), x2_ss.at[n], x2_rs.at[1 - n])])

    pl.when(after_filter)(spread_gas)

    for n in range(2):
        wait_recv((0, (-1, 1)[n], 0), ry_v.at[n, pl.ds(35, 3)], y_rs.at[n, 3])
        wait_recv((0, 0, (-1, 1)[n]), rz_v.at[n, pl.ds(10, 3)], z_rs.at[n, 3])
    for n, (a, b) in enumerate(DIAG):
        wait_recv((0, a, b), rd_v.at[n, pl.ds(5, 3)], d_rs.at[n, 3])

    def shift(j, carry):
        tiles = gas_v[j]
        below, above = ry_v[0, 35 + j], ry_v[1, 35 + j]
        rows = jnp.stack([jnp.where(row0, jnp.broadcast_to(above[i:i + 1], (8, 128)),
                                    jnp.broadcast_to(below[i:i + 1], (8, 128))) for i in range(6)])
        halo_m = jnp.where(col_low, rz_v[0, 10 + j], rz_v[1, 10 + j])
        halo_y = jnp.where(col_low, jnp.where(row0, rd_v[2, 5 + j], rd_v[0, 5 + j]),
                           jnp.where(row0, rd_v[3, 5 + j], rd_v[1, 5 + j]))
        variants = []
        for value, halo in ((tiles, halo_m), (rows, halo_y)):
            edge = unpack(halo, 4, 6)
            variants.append((rot(jnp.where(lane127[None], edge, value), 1, 2), value,
                             rot(jnp.where(lane0[None], edge, value), -1, 2)))
        for c in range(3):
            value, halo = variants[0][c], variants[1][c]
            shifted_v[j, c] = rot(jnp.where(row7[None], halo, value), 1, 1)
            shifted_v[j, 3 + c] = value
            shifted_v[j, 6 + c] = rot(jnp.where(row0[None], halo, value), -1, 1)
        return carry

    lax.fori_loop(0, 3, shift, 0, unroll=True)

    def drag(x, carry):
        totals = [jnp.zeros((4, 8, 128), F32) for _ in range(3)]
        for a in range(3):
            for bc in range(9):
                weight = prod_v[9 * a + bc, :, x]
                for j in range(3):
                    totals[j] = totals[j] + weight * shifted_v[j, bc, x + a][None]
        for j in range(3):
            drag_o[j, :, x] = src_v[1, :, x] * totals[j] - occ_v[:, x] * src_v[2 + j, :, x]
        return carry

    lax.fori_loop(0, 4, drag, 0, unroll=True)

    for n, s in enumerate((-1, 1)):
        wait_recv((s, 0, 0), rx_v.at[n, pl.ds(0, 20)], x_rs.at[n])
        wait_recv((2 * s, 0, 0), rx2_v.at[n], x2_rs.at[n])
    for k in range(5):
        for i in range(4):
            total = filtered_o[k, i] + (rx_v[0, 4 * k + i] + rx_v[1, 4 * k + i])
            if i in (0, 3):
                total = total + rx2_v[i // 3, k]
            filtered_o[k, i] = total

    for n, s in enumerate((-1, 1)):
        wait_send((0, s, 0), sy_v.at[n], y_ss.at[n])
        wait_send((0, 0, s), sz_v.at[n], z_ss.at[n])
        wait_send((s, 0, 0), sx_v.at[n], x_ss.at[n])
        wait_send((2 * s, 0, 0), sx2_v.at[n], x2_ss.at[n])
    for n, (a, b) in enumerate(DIAG):
        wait_send((0, a, b), sd_v.at[n], d_ss.at[n])


def store(filtered_v, drag_v, filtered_h, drag_h, sem):
    copies = [pltpu.make_async_copy(filtered_v, filtered_h, sem.at[0]), pltpu.make_async_copy(drag_v, drag_h, sem.at[1])]
    for item in copies:
        item.start()
    for item in copies:
        item.wait()


def solution(mesh):
    sizes = tuple(mesh.shape[name] for name in ("gx", "gy", "gz"))
    dma = pltpu.SemaphoreType.DMA

    def vmem(*shape):
        return pltpu.VMEM(shape + (8, 128), F32)

    def shards(counts, offsets, volume, beta, particle_velocity, gas_velocity):
        any_space = pl.BlockSpec(memory_space=pl.ANY)
        out_shape = (jax.ShapeDtypeStruct((5, 4, 8, 128), F32), jax.ShapeDtypeStruct((3, 4, 4, 8, 128), F32))
        filtered, drag = pl.pallas_call(
            functools.partial(kernel, sizes),
            out_shape=out_shape,
            in_specs=[any_space] * 6,
            out_specs=(pl.BlockSpec(memory_space=pltpu.VMEM),) * 2,
            scratch_shapes=[
                pltpu.VMEM((4, 8, 128), jnp.int32), vmem(3, 4, 4), vmem(5, 4, 4), vmem(3, 4, 4), vmem(3, 6),
                vmem(4, 4), vmem(27, 4, 4), vmem(3, 9, 6), vmem(5, 6), vmem(5, 6), vmem(5), vmem(5),
                vmem(2, 38), vmem(2, 13), vmem(4, 8), vmem(2, 23), vmem(2, 5),
                vmem(2, 38), vmem(2, 13), vmem(4, 8), vmem(2, 23), vmem(2, 5), vmem(3),
                dma((6,)), dma((2,)), dma((2,)), dma((4,)), dma((2,)), dma((2,)),
                dma((2, 4)), dma((2, 4)), dma((4, 4)), dma((2,)), dma((2,)), dma((2,)), pltpu.SemaphoreType.REGULAR,
            ],
            compiler_params=pltpu.CompilerParams(
                collective_id=0, has_side_effects=True, vmem_limit_bytes=32 * 2**20),
            name="deposit_filter_drag",
        )(*[pltpu.with_memory_space_constraint(v, pltpu.HBM) for v in (
            counts, offsets, volume, beta, particle_velocity, gas_velocity)])
        return pl.pallas_call(
            store, out_shape=out_shape, in_specs=[any_space] * 2, out_specs=(any_space,) * 2,
            scratch_shapes=[dma((2,))], compiler_params=pltpu.CompilerParams(vmem_limit_bytes=2**20), name="store",
        )(filtered, drag)

    in_specs = (
        P("gx", "gy", "gz"),
        P(None, None, "gx", "gy", "gz"),
        P(None, "gx", "gy", "gz"),
        P(None, "gx", "gy", "gz"),
        P(None, None, "gx", "gy", "gz"),
        P(None, "gx", "gy", "gz"),
    )
    out_specs = (P(None, "gx", "gy", "gz"), P(None, None, "gx", "gy", "gz"))
    return jax.shard_map(shards, mesh=mesh, in_specs=in_specs, out_specs=out_specs, check_vma=False)
```

```python
import functools
import math

import jax
import jax.numpy as jnp
import numpy as np
from jax import lax
from jax.experimental import pallas as pl
from jax.experimental.pallas import tpu as pltpu
from jax.sharding import PartitionSpec as P

MESH = pl.DeviceIdType.MESH
F32 = jnp.float32
SIGMA = 0.6
INV_S2 = 1.0 / (SIGMA * SIGMA)
CENTRE = math.exp(0.5 * INV_S2)
ITERS = 4
FILTER = 2.0

SIDES = ((1, 0), (0, 1), (1, 1))
DIAG = ((-1, -1), (-1, 1), (1, -1), (1, 1))
ALL = ([(0, a, b) for a in (-1, 0, 1) for b in (-1, 0, 1) if (a, b) != (0, 0)]
       + [(-1, 0, 0), (1, 0, 0), (-2, 0, 0), (2, 0, 0)])


def filter_taps():
    unit = np.zeros((2 * ITERS + 3,) * 3)
    unit[(ITERS + 1,) * 3] = 1.0
    current = unit
    for _ in range(ITERS):
        around = sum(np.roll(current, step, axis) for axis in range(3) for step in (-1, 1))
        current = (unit + FILTER * around) / (1.0 + 6.0 * FILTER)
    return current[ITERS + 1:, ITERS + 1:, ITERS + 1:]


TAPS = filter_taps()


def rot(value, shift, axis):
    size = value.shape[axis]
    return pltpu.roll(value, shift % size, axis)


def kernel(sizes, counts_h, offsets_h, volume_h, beta_h, pv_h, gas_h, filtered_o, drag_o,
           counts_v, offsets_v, src_v, pv_v, gas_v, occ_v, prod_v, shifted_v, dm_v, dy_v, dz_v, dyz_v,
           sy_v, sz_v, sd_v, sx_v, sx2_v, ry_v, rz_v, rd_v, rx_v, rx2_v, sgz_v, by_v, bz_v, bd_v, rg_v,
           in_sem, y_ss, z_ss, d_ss, x_ss, x2_ss, y_rs, z_rs, d_rs, gx_rs, x_rs, x2_rs, late_sem, b_rs, pg_ss, pg_rs):
    me = (lax.axis_index("gx"), lax.axis_index("gy"), lax.axis_index("gz"))

    def near(step):
        place = tuple(me[i] + step[i] for i in range(3))
        ok = None
        for i in range(3):
            if step[i]:
                inside = place[i] >= 0 if step[i] < 0 else place[i] < sizes[i]
                ok = inside if ok is None else ok & inside
        origin = None
        if max(step) <= 0:
            origin = (place[0] == 0) & (place[1] == 0) & (place[2] == 0)
        return place, ok, origin

    def copy(step, src, dst, ssem, rsem):
        return pltpu.make_async_remote_copy(src_ref=src, dst_ref=dst, send_sem=ssem, recv_sem=rsem,
                                            device_id=near(step)[0], device_id_type=MESH)

    def send(items, to_origin=None):
        _, ok, origin = near(items[0][0])
        if to_origin is not None and origin is not None:
            ok = origin if to_origin else ok & jnp.logical_not(origin)
        elif to_origin:
            return

        @pl.when(ok)
        def _():
            for item in items:
                copy(*item).start()

    def wait_recv(step, dst, rsem):
        @pl.when(near(step)[1])
        def _():
            copy(step, dst, dst, rsem, rsem).wait_recv()

    def wait_send(step, src, ssem):
        @pl.when(near(step)[1])
        def _():
            copy(step, src, src, ssem, ssem).wait_send()

    def at(*place):
        return (me[0] == place[0]) & (me[1] == place[1]) & (me[2] == place[2])

    is_origin, is_proxy = at(0, 0, 0), at(1, 0, 0)
    is_beside = at(0, 1, 0) | at(0, 0, 1) | at(0, 1, 1)
    barrier = pltpu.get_barrier_semaphore()
    late = [step for step in ALL if min(step) >= 0]

    @pl.when(is_origin)
    def _():
        pl.semaphore_wait(barrier, len(late))
        for step in late:
            pl.semaphore_signal(late_sem, inc=1, device_id=step, device_id_type=MESH)

    loads = [
        pltpu.make_async_copy(offsets_h, offsets_v, in_sem.at[0]),
        pltpu.make_async_copy(counts_h, counts_v, in_sem.at[1]),
        pltpu.make_async_copy(gas_h, gas_v.at[:, pl.ds(1, 4)], in_sem.at[2]),
        pltpu.make_async_copy(volume_h, src_v.at[0], in_sem.at[3]),
        pltpu.make_async_copy(beta_h, src_v.at[1], in_sem.at[4]),
        pltpu.make_async_copy(pv_h, pv_v, in_sem.at[5]),
    ]
    for load in loads:
        load.start()

    greeted = jnp.int32(0)
    for step in ALL:
        _, ok, origin = near(step)
        greets = ok if origin is None else ok & jnp.logical_not(origin)
        greeted = greeted + greets.astype(jnp.int32)
    greeted = greeted + 3 * is_proxy.astype(jnp.int32) + is_beside.astype(jnp.int32)

    @pl.when(is_beside)
    def _():
        pl.semaphore_signal(barrier, inc=1, device_id=(1, 0, 0), device_id_type=MESH)

    @pl.when(is_proxy)
    def _():
        for a, b in SIDES:
            pl.semaphore_signal(barrier, inc=1, device_id=(0, a, b), device_id_type=MESH)

    @pl.when(jnp.logical_not(is_origin))
    def _():
        for step in ALL:
            place, ok, _ = near(step)

            @pl.when(ok)
            def _():
                pl.semaphore_signal(barrier, inc=1, device_id=place, device_id_type=MESH)

    def clear(step, refs):
        @pl.when(jnp.logical_not(near(step)[1]))
        def _():
            for ref in refs:
                ref[...] = jnp.zeros(ref.shape, F32)

    for n, s in enumerate((-1, 1)):
        clear((s, 0, 0), [rx_v.at[n]])
        clear((2 * s, 0, 0), [rx2_v.at[n]])
        clear((0, s, 0), [ry_v.at[n]])
        clear((0, 0, s), [rz_v.at[n]])
    for n, (a, b) in enumerate(DIAG):
        clear((0, a, b), [rd_v.at[n]])

    def fill(which, refs):
        @pl.when(which)
        def _():
            for ref in refs:
                ref[...] = jnp.zeros(ref.shape, F32)

    fill(is_origin, [ry_v.at[1, pl.ds(0, 35)], rz_v.at[1, pl.ds(0, 10)], rd_v.at[3, pl.ds(0, 5)],
                     gas_v.at[:, 0], gas_v.at[:, 5]])

    row = lax.broadcasted_iota(jnp.int32, (8, 128), 0)
    lane = lax.broadcasted_iota(jnp.int32, (8, 128), 1)
    slot, col = lane >> 3, lane & 7
    row0, row7, row_low = row == 0, row == 7, row < 4
    lane0, lane127, col_low = lane == 0, lane == 127, col < 4

    edge_rows = (row_low & (me[1] == sizes[1] - 1)) | (~row_low & (me[1] == 0))
    edge_cols = (col_low & (me[2] == 0)) | (~col_low & (me[2] == sizes[2] - 1))
    keep_first, keep_last = (me[0] > 0).astype(F32), (me[0] < sizes[0] - 1).astype(F32)

    def mirror_rows(tiles, spill):
        image = jnp.where((row == 1) | (row == 4), rot(tiles, 2, tiles.ndim - 2), jnp.where(
            (row == 2) | (row == 5), rot(tiles, 4, tiles.ndim - 2),
            jnp.where((row == 3) | (row == 6), rot(tiles, 6, tiles.ndim - 2), 0.0)))
        return jnp.where(edge_rows, -image, spill)

    def mirror_cols(packed, spill):
        image = jnp.where(col == 0, rot(packed, -6, 1), jnp.where(col == 1, rot(packed, -4, 1), jnp.where(
            col == 2, rot(packed, -2, 1), jnp.where(col == 5, rot(packed, 2, 1), jnp.where(
                col == 6, rot(packed, 4, 1), jnp.where(col == 7, rot(packed, 6, 1), 0.0))))))
        return jnp.where(edge_cols, -image, spill)

    def part(n, ref, per, g):
        return ref.at[n, pl.ds(2 * per * g, per if isinstance(g, int) and g == 2 else 2 * per)]

    def gas_x(n):
        return ((-1, 1)[n], 0, 0), sx_v.at[n, pl.ds(20, 3)], rx_v.at[1 - n, pl.ds(20, 3)], x_ss.at[n], gx_rs.at[1 - n]

    def send_gas_x(to_origin):
        for n in range(2):
            send([gas_x(n)], to_origin)

    def send_group(g, to_origin):
        for n, (a, b) in enumerate(DIAG):
            send([((0, a, b), part(n, sd_v, 1, g), part(3 - n, rd_v, 1, g), d_ss.at[n], d_rs.at[3 - n, g])], to_origin)
        for n in range(2):
            send([((0, 0, (-1, 1)[n]), part(n, sz_v, 2, g), part(1 - n, rz_v, 2, g), z_ss.at[n], z_rs.at[1 - n, g])],
                 to_origin)
            send([((0, (-1, 1)[n], 0), part(n, sy_v, 7, g), part(1 - n, ry_v, 7, g), y_ss.at[n], y_rs.at[1 - n, g])],
                 to_origin)

    def wait_group(g):
        @pl.when(jnp.logical_not(is_origin))
        def _():
            for n in range(2):
                wait_recv((0, (-1, 1)[n], 0), part(n, ry_v, 7, g), y_rs.at[n, g])
                wait_recv((0, 0, (-1, 1)[n]), part(n, rz_v, 2, g), z_rs.at[n, g])
            for n, (a, b) in enumerate(DIAG):
                wait_recv((0, a, b), part(n, rd_v, 1, g), d_rs.at[n, g])

    def take_gas(n):
        wait_recv(((-1, 1)[n], 0, 0), rx_v.at[n, pl.ds(20, 3)], gx_rs.at[n])
        for j in range(3):
            gas_v[j, 5 * n] = rx_v[n, 20 + j]

    def pack(planes, first):
        result = jnp.zeros((8, 128), F32)
        for i in range(planes.shape[0]):
            result = jnp.where(slot == first + i, rot(planes[i], 8 * (first + i) + 4, 1), result)
        return result

    def spread_gas():
        for j in range(3):
            sgz_v[j] = pack(gas_v[j], 4)
            for i in range(6):
                sy_v[0, 35 + j, pl.ds(i, 1), :] = gas_v[j, i, pl.ds(0, 1), :]
                sy_v[1, 35 + j, pl.ds(i, 1), :] = gas_v[j, i, pl.ds(7, 1), :]
            for n in range(2):
                sy_v[n, 35 + j, pl.ds(6, 2), :] = jnp.zeros((2, 128), F32)
        for n in range(2):
            send([((0, (-1, 1)[n], 0), sy_v.at[n, pl.ds(35, 3)], ry_v.at[1 - n, pl.ds(35, 3)], y_ss.at[n], y_rs.at[1 - n, 3])])
            send([((0, 0, (-1, 1)[n]), sgz_v, rz_v.at[1 - n, pl.ds(10, 3)], z_ss.at[n], z_rs.at[1 - n, 3])])
        for n, (a, b) in enumerate(DIAG):
            send([((0, a, b), sgz_v, rd_v.at[3 - n, pl.ds(5, 3)], d_ss.at[n], d_rs.at[3 - n, 3])])

    loads[0].wait()
    loads[1].wait()

    def products(s, carry):
        occ = jnp.where(counts_v[...] > s, F32(1.0), F32(0.0))
        occ_v[s] = occ
        weights, norm = [], None
        for axis in range(3):
            t = jnp.exp((0.5 - offsets_v[axis, s]) * INV_S2)
            low, mid = t * t, CENTRE * t
            total = low + mid + 1.0
            norm = total if norm is None else norm * total
            weights.append((low, mid))
        scale = occ / norm
        wx = (weights[0][0] * scale, weights[0][1] * scale, scale)
        for a in range(3):
            for b in range(3):
                xy = wx[a] * weights[1][b] if b < 2 else wx[a]
                for c in range(3):
                    prod_v[9 * a + 3 * b + c, s] = xy * weights[2][c] if c < 2 else xy
        return carry

    lax.fori_loop(0, 4, products, 0, unroll=True)
    loads[2].wait()
    for j in range(3):
        sx_v[0, 20 + j] = gas_v[j, 1]
        sx_v[1, 20 + j] = gas_v[j, 4]

    @pl.when(is_origin)
    def _():
        send_gas_x(None)
        spread_gas()

    for load in loads[3:]:
        load.wait()
    for j in range(3):
        src_v[2 + j] = src_v[1] * pv_v[j]

    def unpack(tile, first, count):
        return jnp.stack([rot(tile, -(8 * (first + i) + 4), 1) for i in range(count)])

    def deposit(k, carry):
        src = [src_v[k, s] for s in range(4)]
        by_z = []
        for c in range(3):
            by_y = []
            for b in range(3):
                by_x = []
                for a in range(3):
                    total = src[0] * prod_v[9 * a + 3 * b + c, 0]
                    for s in range(1, 4):
                        total = total + src[s] * prod_v[9 * a + 3 * b + c, s]
                    by_x.append(total)
                lo, mid, hi = by_x
                by_y.append(jnp.concatenate([
                    lo[0:1], lo[1:2] + mid[0:1], lo[2:4] + mid[1:3] + hi[0:2], mid[3:4] + hi[2:3], hi[3:4]], axis=0))
            up, down = rot(by_y[2], 1, 1), rot(by_y[0], -1, 1)
            by_z.append((by_y[1] + jnp.where(row0, 0.0, up) + jnp.where(row7, 0.0, down),
                         jnp.where(row0, up, jnp.where(row7, down, 0.0))))
        main, packs = [], []
        for kind in range(2):
            up, down = rot(by_z[2][kind], 1, 2), rot(by_z[0][kind], -1, 2)
            spill = jnp.where(lane0, up, jnp.where(lane127, down, 0.0))
            main.append(by_z[1][kind] + jnp.where(lane0, 0.0, up) + jnp.where(lane127, 0.0, down))
            packed = rot(spill[0], 36, 1) * keep_first
            for i in range(1, 5):
                packed = packed + rot(spill[i], 8 * i + 36, 1)
            packs.append(packed + rot(spill[5], 76, 1) * keep_last)
        m, y = [jnp.concatenate([v[0:1] * keep_first, v[1:5], v[5:6] * keep_last], axis=0) for v in main]
        z, yz = packs
        y, yz = mirror_rows(m, y), mirror_rows(z, yz)
        mp, yp = pack(m, 4), pack(y, 4)
        z, yz = mirror_cols(mp, z), mirror_cols(yp, yz)
        dm_v[k], dy_v[k], dz_v[k], dyz_v[k] = m, y, z, yz
        sy_v[0, pl.ds(7 * k, 6)] = jnp.where(row_low, m, y)
        sy_v[1, pl.ds(7 * k, 6)] = jnp.where(row_low, y, m)
        sy_v[0, 7 * k + 6] = jnp.where(row_low, z, yz)
        sy_v[1, 7 * k + 6] = jnp.where(row_low, yz, z)
        zm = (jnp.where(col_low, z, mp), jnp.where(col_low, mp, z))
        zy = (jnp.where(col_low, yz, yp), jnp.where(col_low, yp, yz))
        for n in range(2):
            sz_v[n, 2 * k], sz_v[n, 2 * k + 1] = zm[n], zy[n]
        for n, (a, b) in enumerate(DIAG):
            first, second = (zm, zy) if a < 0 else (zy, zm)
            sd_v[n, k] = jnp.where(row_low, first[(b + 1) // 2], second[(b + 1) // 2])
        return carry

    def deposit_two(g, carry):
        deposit(2 * g, carry)
        deposit(2 * g + 1, carry)

        @pl.when(is_origin)
        def _():
            send_group(g, None)

        return carry

    lax.fori_loop(0, 2, deposit_two, 0)
    deposit(4, 0)

    @pl.when(is_origin)
    def _():
        send_group(2, None)

    @pl.when(jnp.logical_not(is_origin))
    def _():
        pl.semaphore_wait(barrier, greeted)
        send_gas_x(False)
        for g in range(3):
            send_group(g, False)

    to_proxy = [(at(0, a, b), copy((1, -a, -b), src, dst, ssem, b_rs.at[n]))
                for n, ((a, b), src, dst, ssem) in enumerate((
                    (SIDES[0], sy_v.at[0, pl.ds(0, 35)], by_v, y_ss.at[0]),
                    (SIDES[1], sz_v.at[0, pl.ds(0, 10)], bz_v, z_ss.at[0]),
                    (SIDES[2], sd_v.at[0, pl.ds(0, 5)], bd_v, d_ss.at[0])))]
    for here, item in to_proxy:
        pl.when(here)(item.start)

    @pl.when(is_proxy)
    def _():
        for a, b in SIDES:
            copy((-1, a, b), sx_v.at[0, pl.ds(20, 3)], rg_v, pg_ss, pg_rs).start()

    by_origin = jnp.bool_(False)
    for step in ALL:
        if max(step) <= 0:
            by_origin = by_origin | near(step)[2]

    @pl.when(by_origin & jnp.logical_not(is_proxy))
    def _():
        pl.semaphore_wait(late_sem, 1)

    @pl.when(jnp.logical_not(is_origin | is_proxy))
    def _():
        take_gas(0)
        take_gas(1)
        spread_gas()


    def convolve(m, y, z, yz):
        edge_m, edge_y = unpack(z, 4, 6), unpack(yz, 4, 6)
        parts = [None] * 5

        def add(sum_s, sum_c, value):
            for d in range(5 - sum_s - sum_c):
                term = value * F32(TAPS[d, sum_s, sum_c])
                parts[d] = term if parts[d] is None else parts[d] + term

        for c in range(5):
            rows = []
            for kind, (tiles, edge) in enumerate(((m, edge_m), (y, edge_y))):
                if c and not (kind and c == 4):
                    tiles = (rot(jnp.where(lane < c, edge, tiles), -c, 2)
                             + rot(jnp.where(lane >= 128 - c, edge, tiles), c, 2))
                rows.append(tiles)
            add(0, c, rows[0])
            for s in range(1, 5 - c):
                add(s, c, rot(jnp.where(row < s, rows[1], rows[0]), -s, 1)
                    + rot(jnp.where(row >= 8 - s, rows[1], rows[0]), s, 1))
        pushed = [None] * 14
        for i in range(6):
            for d in range(5):
                for q in {i + 4 - d, i + 4 + d}:
                    pushed[q] = parts[d][i] if pushed[q] is None else pushed[q] + parts[d][i]
        return pushed

    row_in, col_in = ~row_low, ~col_low
    ends = (lane0 | lane127)[None]

    def around(k):
        tiles, halo, diag = by_v[pl.ds(7 * k, 6)], by_v[7 * k + 6], bd_v[k]
        low_m = bz_v[2 * k] + jnp.where(row_in, diag, 0.0)
        low_y = bz_v[2 * k + 1] + jnp.where(row_in, 0.0, diag)
        m = jnp.where(row_in[None], tiles, 0.0) + jnp.where(ends, unpack(jnp.where(col_in, 0.0, low_m), 4, 6), 0.0)
        y = jnp.where(row_in[None], 0.0, tiles) + jnp.where(ends, unpack(jnp.where(col_in, 0.0, low_y), 4, 6), 0.0)
        z = jnp.where(row_in, halo, 0.0) + jnp.where(col_in, low_m, 0.0)
        yz = jnp.where(row_in, 0.0, halo) + jnp.where(col_in, low_y, 0.0)
        pushed = convolve(m, y, z, yz)
        own = [pushed[5 + i] - pushed[3 - i] for i in range(3)] + [pushed[8]]
        return own, pushed[9:13], pushed[13]

    def filter_one(k, carry):
        below, above = ry_v[0, pl.ds(7 * k, 6)], ry_v[1, pl.ds(7 * k, 6)]
        below_z, above_z = ry_v[0, 7 * k + 6], ry_v[1, 7 * k + 6]
        m = dm_v[k] + jnp.where(row_low[None], below, above)
        y = dy_v[k] + jnp.where(row_low[None], above, below)
        side = []
        for n, b in enumerate((0, 1)):
            lower, upper = rd_v[b, k], rd_v[2 + b, k]
            side.append((rz_v[n, 2 * k] + jnp.where(row_low, lower, upper),
                         rz_v[n, 2 * k + 1] + jnp.where(row_low, upper, lower)))
        z = dz_v[k] + jnp.where(col_low, side[0][0], side[1][0]) + jnp.where(row_low, below_z, above_z)
        yz = dyz_v[k] + jnp.where(col_low, side[0][1], side[1][1]) + jnp.where(row_low, above_z, below_z)
        m = m + jnp.where(ends, unpack(jnp.where(col_low, side[1][0], side[0][0]), 4, 6), 0.0)
        y = y + jnp.where(ends, unpack(jnp.where(col_low, side[1][1], side[0][1]), 4, 6), 0.0)
        pushed = convolve(m, y, z, yz)
        for i in range(4):
            sx_v[0, 4 * k + i] = pushed[1 + i]
            filtered_o[k, i] = pushed[5 + i]
            sx_v[1, 4 * k + i] = pushed[9 + i]
        sx2_v[0, k] = pushed[0]
        sx2_v[1, k] = pushed[13]

        @pl.when(me[0] == 0)
        def _():
            for i in range(3):
                rx_v[0, 4 * k + i] = -pushed[3 - i]

        @pl.when(me[0] == sizes[0] - 1)
        def _():
            for i in range(1, 4):
                rx_v[1, 4 * k + i] = -pushed[13 - i]
        return carry

    def push(first, count, to_origin=None):
        for n, s in enumerate((-1, 1)):
            tiles = pl.ds(4 * first, 4 * count)
            send([((s, 0, 0), sx_v.at[n, tiles], rx_v.at[1 - n, tiles], x_ss.at[n], x_rs.at[1 - n])], to_origin)

    def push_far(to_origin=None):
        for n, s in enumerate((-1, 1)):
            send([((2 * s, 0, 0), sx2_v.at[n], rx2_v.at[1 - n], x2_ss.at[n], x2_rs.at[1 - n])], to_origin)

    def filter_and_push(k, carry):
        filter_one(k, carry)

        @pl.when(jnp.logical_not(is_proxy))
        def _():
            push(k, 1)

        return carry

    def filter_two(g, carry):
        wait_group(g)
        filter_and_push(2 * g, carry)
        filter_and_push(2 * g + 1, carry)
        return carry

    lax.fori_loop(0, 2, filter_two, 0)
    wait_group(2)
    filter_and_push(4, 0)

    @pl.when(jnp.logical_not(is_proxy))
    def _():
        push_far()

    def around_one(k, carry):
        @pl.when((k == 0) & is_proxy)
        def _():
            for n, dst in enumerate((by_v, bz_v, bd_v)):
                copy((-1, 0, 0), dst, dst, b_rs.at[n], b_rs.at[n]).wait_recv()

        @pl.when(is_proxy)
        def _():
            own, right, far = around(k)
            for i in range(4):
                filtered_o[k, i] += right[i]
                sx_v[0, 4 * k + i] += own[i]
            sx_v[1, 4 * k] += far

        return carry

    lax.fori_loop(0, 5, around_one, 0)

    @pl.when(is_proxy)
    def _():
        push(0, 5, False)
        push_far(False)
        pl.semaphore_wait(late_sem, 1)
        send_gas_x(True)
        push(0, 5, True)
        push_far(True)

    @pl.when(is_origin)
    def _():
        take_gas(1)

    @pl.when(is_proxy)
    def _():
        take_gas(0)
        take_gas(1)
        spread_gas()


    for n in range(2):
        wait_recv((0, (-1, 1)[n], 0), ry_v.at[n, pl.ds(35, 3)], y_rs.at[n, 3])
        wait_recv((0, 0, (-1, 1)[n]), rz_v.at[n, pl.ds(10, 3)], z_rs.at[n, 3])
    for n, (a, b) in enumerate(DIAG):
        wait_recv((0, a, b), rd_v.at[n, pl.ds(5, 3)], d_rs.at[n, 3])

    @pl.when(is_beside)
    def _():
        copy((1, 0, 0), rg_v, rg_v, pg_rs, pg_rs).wait_recv()

    @pl.when(at(0, 1, 0))
    def _():
        for j in range(3):
            ry_v[0, 35 + j, pl.ds(5, 1), :] = rg_v[j, pl.ds(7, 1), :]

    for y, ref, tile in ((0, rz_v, 10), (1, rd_v, 5)):
        @pl.when(at(0, y, 1))
        def _():
            for j in range(3):
                ref[0, tile + j] = jnp.where(slot == 9, rot(rg_v[j], 76, 1), ref[0, tile + j])

    def shift(j, carry):
        tiles = gas_v[j]
        below, above = ry_v[0, 35 + j], ry_v[1, 35 + j]
        rows = jnp.stack([jnp.where(row0, jnp.broadcast_to(above[i:i + 1], (8, 128)),
                                    jnp.broadcast_to(below[i:i + 1], (8, 128))) for i in range(6)])
        halo_m = jnp.where(col_low, rz_v[0, 10 + j], rz_v[1, 10 + j])
        halo_y = jnp.where(col_low, jnp.where(row0, rd_v[2, 5 + j], rd_v[0, 5 + j]),
                           jnp.where(row0, rd_v[3, 5 + j], rd_v[1, 5 + j]))
        variants = []
        for value, halo in ((tiles, halo_m), (rows, halo_y)):
            edge = unpack(halo, 4, 6)
            variants.append((rot(jnp.where(lane127[None], edge, value), 1, 2), value,
                             rot(jnp.where(lane0[None], edge, value), -1, 2)))
        for c in range(3):
            value, halo = variants[0][c], variants[1][c]
            shifted_v[j, c] = rot(jnp.where(row7[None], halo, value), 1, 1)
            shifted_v[j, 3 + c] = value
            shifted_v[j, 6 + c] = rot(jnp.where(row0[None], halo, value), -1, 1)
        return carry

    lax.fori_loop(0, 3, shift, 0, unroll=True)

    def drag(x, carry):
        totals = [jnp.zeros((4, 8, 128), F32) for _ in range(3)]
        for a in range(3):
            for bc in range(9):
                weight = prod_v[9 * a + bc, :, x]
                for j in range(3):
                    totals[j] = totals[j] + weight * shifted_v[j, bc, x + a][None]
        for j in range(3):
            drag_o[j, :, x] = src_v[1, :, x] * totals[j] - occ_v[:, x] * src_v[2 + j, :, x]
        return carry

    lax.fori_loop(0, 4, drag, 0, unroll=True)

    for n, s in enumerate((-1, 1)):
        wait_recv((s, 0, 0), rx_v.at[n, pl.ds(0, 20)], x_rs.at[n])
        wait_recv((2 * s, 0, 0), rx2_v.at[n], x2_rs.at[n])
    for k in range(5):
        for i in range(4):
            total = filtered_o[k, i] + (rx_v[0, 4 * k + i] + rx_v[1, 4 * k + i])
            if i in (0, 3):
                total = total + rx2_v[i // 3, k]
            filtered_o[k, i] = total

    for n, s in enumerate((-1, 1)):
        wait_send((s, 0, 0), sx_v.at[n], x_ss.at[n])
        wait_send((2 * s, 0, 0), sx2_v.at[n], x2_ss.at[n])

    for n, s in enumerate((-1, 1)):
        wait_send((0, s, 0), sy_v.at[n], y_ss.at[n])
        wait_send((0, 0, s), sz_v.at[n], z_ss.at[n])
    for n, (a, b) in enumerate(DIAG):
        wait_send((0, a, b), sd_v.at[n], d_ss.at[n])

    @pl.when(is_proxy)
    def _():
        nine = sx_v.at[0, pl.ds(0, 9)]
        copy((1, 0, 0), nine, nine, pg_ss, pg_ss).wait_send()


def store(filtered_v, drag_v, filtered_h, drag_h, sem):
    copies = [pltpu.make_async_copy(filtered_v, filtered_h, sem.at[0]), pltpu.make_async_copy(drag_v, drag_h, sem.at[1])]
    for item in copies:
        item.start()
    for item in copies:
        item.wait()


def solution(mesh):
    sizes = tuple(mesh.shape[name] for name in ("gx", "gy", "gz"))
    dma = pltpu.SemaphoreType.DMA

    def vmem(*shape):
        return pltpu.VMEM(shape + (8, 128), F32)

    def shards(counts, offsets, volume, beta, particle_velocity, gas_velocity):
        any_space = pl.BlockSpec(memory_space=pl.ANY)
        out_shape = (jax.ShapeDtypeStruct((5, 4, 8, 128), F32), jax.ShapeDtypeStruct((3, 4, 4, 8, 128), F32))
        filtered, drag = pl.pallas_call(
            functools.partial(kernel, sizes),
            out_shape=out_shape,
            in_specs=[any_space] * 6,
            out_specs=(pl.BlockSpec(memory_space=pltpu.VMEM),) * 2,
            scratch_shapes=[
                pltpu.VMEM((4, 8, 128), jnp.int32), vmem(3, 4, 4), vmem(5, 4, 4), vmem(3, 4, 4), vmem(3, 6),
                vmem(4, 4), vmem(27, 4, 4), vmem(3, 9, 6), vmem(5, 6), vmem(5, 6), vmem(5), vmem(5),
                vmem(2, 38), vmem(2, 13), vmem(4, 8), vmem(2, 23), vmem(2, 5),
                vmem(2, 38), vmem(2, 13), vmem(4, 8), vmem(2, 23), vmem(2, 5), vmem(3),
                vmem(35), vmem(10), vmem(5), vmem(3),
                dma((6,)), dma((2,)), dma((2,)), dma((4,)), dma((2,)), dma((2,)),
                dma((2, 4)), dma((2, 4)), dma((4, 4)), dma((2,)), dma((2,)), dma((2,)), pltpu.SemaphoreType.REGULAR,
                dma((3,)), dma, dma,
            ],
            compiler_params=pltpu.CompilerParams(
                collective_id=0, has_side_effects=True, vmem_limit_bytes=32 * 2**20),
            name="deposit_filter_drag",
        )(*[pltpu.with_memory_space_constraint(v, pltpu.HBM) for v in (
            counts, offsets, volume, beta, particle_velocity, gas_velocity)])
        return pl.pallas_call(
            store, out_shape=out_shape, in_specs=[any_space] * 2, out_specs=(any_space,) * 2,
            scratch_shapes=[dma((2,))], compiler_params=pltpu.CompilerParams(vmem_limit_bytes=2**20), name="store",
        )(filtered, drag)

    in_specs = (
        P("gx", "gy", "gz"),
        P(None, None, "gx", "gy", "gz"),
        P(None, "gx", "gy", "gz"),
        P(None, "gx", "gy", "gz"),
        P(None, None, "gx", "gy", "gz"),
        P(None, "gx", "gy", "gz"),
    )
    out_specs = (P(None, "gx", "gy", "gz"), P(None, None, "gx", "gy", "gz"))
    return jax.shard_map(shards, mesh=mesh, in_specs=in_specs, out_specs=out_specs, check_vma=False)
```

```python
import functools
import math

import jax
import jax.numpy as jnp
import numpy as np
from jax import lax
from jax.experimental import pallas as pl
from jax.experimental.pallas import tpu as pltpu
from jax.sharding import PartitionSpec as P

MESH = pl.DeviceIdType.MESH
F32 = jnp.float32
SIGMA = 0.6
INV_S2 = 1.0 / (SIGMA * SIGMA)
CENTRE = math.exp(0.5 * INV_S2)
ITERS = 4
FILTER = 2.0

SIDES = ((1, 0), (0, 1), (1, 1))
DIAG = ((-1, -1), (-1, 1), (1, -1), (1, 1))
ALL = ([(0, a, b) for a in (-1, 0, 1) for b in (-1, 0, 1) if (a, b) != (0, 0)]
       + [(-1, 0, 0), (1, 0, 0), (-2, 0, 0), (2, 0, 0)])


def filter_taps():
    unit = np.zeros((2 * ITERS + 3,) * 3)
    unit[(ITERS + 1,) * 3] = 1.0
    current = unit
    for _ in range(ITERS):
        around = sum(np.roll(current, step, axis) for axis in range(3) for step in (-1, 1))
        current = (unit + FILTER * around) / (1.0 + 6.0 * FILTER)
    return current[ITERS + 1:, ITERS + 1:, ITERS + 1:]


TAPS = filter_taps()


def rot(value, shift, axis):
    size = value.shape[axis]
    return pltpu.roll(value, shift % size, axis)


def kernel(sizes, counts_h, offsets_h, volume_h, beta_h, pv_h, gas_h, filtered_o, drag_o,
           counts_v, offsets_v, src_v, pv_v, gas_v, occ_v, prod_v, shifted_v, dm_v, dy_v, dz_v, dyz_v,
           sy_v, sz_v, sd_v, sx_v, sx2_v, ry_v, rz_v, rd_v, rx_v, rx2_v, sgz_v, by_v, bz_v, bd_v, rg_v,
           in_sem, y_ss, z_ss, d_ss, x_ss, x2_ss, y_rs, z_rs, d_rs, gx_rs, x_rs, x2_rs, late_sem, b_rs, o_ss, pg_ss, pg_rs):
    me = (lax.axis_index("gx"), lax.axis_index("gy"), lax.axis_index("gz"))

    def near(step):
        place = tuple(me[i] + step[i] for i in range(3))
        ok = None
        for i in range(3):
            if step[i]:
                inside = place[i] >= 0 if step[i] < 0 else place[i] < sizes[i]
                ok = inside if ok is None else ok & inside
        origin = None
        if max(step) <= 0:
            origin = (place[0] == 0) & (place[1] == 0) & (place[2] == 0)
        return place, ok, origin

    def copy(step, src, dst, ssem, rsem):
        return pltpu.make_async_remote_copy(src_ref=src, dst_ref=dst, send_sem=ssem, recv_sem=rsem,
                                            device_id=near(step)[0], device_id_type=MESH)

    def send(items, to_origin=None):
        _, ok, origin = near(items[0][0])
        if to_origin is not None and origin is not None:
            ok = origin if to_origin else ok & jnp.logical_not(origin)
        elif to_origin:
            return

        @pl.when(ok)
        def _():
            for item in items:
                copy(*item).start()

    def wait_recv(step, dst, rsem):
        @pl.when(near(step)[1])
        def _():
            copy(step, dst, dst, rsem, rsem).wait_recv()

    def wait_send(step, src, ssem):
        @pl.when(near(step)[1])
        def _():
            copy(step, src, src, ssem, ssem).wait_send()

    def at(*place):
        return (me[0] == place[0]) & (me[1] == place[1]) & (me[2] == place[2])

    is_origin, is_proxy = at(0, 0, 0), at(1, 0, 0)
    is_late = [(me[0] == x) & (me[1] <= 1) & (me[2] == 1) for x in range(3)]
    is_beside = [is_late[x] | at(x, 1, 0) for x in range(2)]
    barrier = pltpu.get_barrier_semaphore()
    late = [step for step in ALL if min(step) >= 0]

    @pl.when(is_origin)
    def _():
        pl.semaphore_wait(barrier, len(late) + 5)
        for step in late:
            pl.semaphore_signal(late_sem, inc=1, device_id=step, device_id_type=MESH)

    loads = [
        pltpu.make_async_copy(offsets_h, offsets_v, in_sem.at[0]),
        pltpu.make_async_copy(counts_h, counts_v, in_sem.at[1]),
        pltpu.make_async_copy(gas_h, gas_v.at[:, pl.ds(1, 4)], in_sem.at[2]),
        pltpu.make_async_copy(volume_h, src_v.at[0], in_sem.at[3]),
        pltpu.make_async_copy(beta_h, src_v.at[1], in_sem.at[4]),
        pltpu.make_async_copy(pv_h, pv_v, in_sem.at[5]),
    ]
    for load in loads:
        load.start()

    greeted = jnp.int32(0)
    for step in ALL:
        _, ok, origin = near(step)
        greets = ok if origin is None else ok & jnp.logical_not(origin)
        greeted = greeted + greets.astype(jnp.int32)
    greeted = greeted + 3 * is_proxy.astype(jnp.int32) + is_beside[0].astype(jnp.int32)

    @pl.when(is_beside[1] | is_late[2])
    def _():
        pl.semaphore_signal(barrier, inc=1, device_id=(0, 0, 0), device_id_type=MESH)

    @pl.when(is_beside[0])
    def _():
        pl.semaphore_signal(barrier, inc=1, device_id=(1, 0, 0), device_id_type=MESH)

    @pl.when(is_proxy)
    def _():
        for a, b in SIDES:
            pl.semaphore_signal(barrier, inc=1, device_id=(0, a, b), device_id_type=MESH)

    @pl.when(jnp.logical_not(is_origin))
    def _():
        for step in ALL:
            place, ok, _ = near(step)

            @pl.when(ok)
            def _():
                pl.semaphore_signal(barrier, inc=1, device_id=place, device_id_type=MESH)

    def clear(step, refs):
        @pl.when(jnp.logical_not(near(step)[1]))
        def _():
            for ref in refs:
                ref[...] = jnp.zeros(ref.shape, F32)

    for n, s in enumerate((-1, 1)):
        clear((s, 0, 0), [rx_v.at[n]])
        clear((2 * s, 0, 0), [rx2_v.at[n]])
        clear((0, s, 0), [ry_v.at[n]])
        clear((0, 0, s), [rz_v.at[n]])
    for n, (a, b) in enumerate(DIAG):
        clear((0, a, b), [rd_v.at[n]])

    def fill(which, refs):
        @pl.when(which)
        def _():
            for ref in refs:
                ref[...] = jnp.zeros(ref.shape, F32)

    fill(is_origin, [ry_v.at[1, pl.ds(0, 35)], rz_v.at[1, pl.ds(0, 10)], rd_v.at[3, pl.ds(0, 5)],
                     gas_v.at[:, 0], gas_v.at[:, 5]])
    fill(is_proxy, [gas_v.at[:, 0]])
    fill(at(0, 0, 1), [rz_v.at[0, pl.ds(0, 10)]])
    fill(at(0, 1, 1), [rd_v.at[0, pl.ds(0, 5)]])
    fill(is_late[0] | is_late[1], [by_v])
    fill((is_late[0] | is_late[1] | is_late[2]) & (me[1] == 0), [bd_v])
    fill((is_late[0] | is_late[1] | is_late[2]) & (me[1] == 1), [bz_v])

    row = lax.broadcasted_iota(jnp.int32, (8, 128), 0)
    lane = lax.broadcasted_iota(jnp.int32, (8, 128), 1)
    slot, col = lane >> 3, lane & 7
    row0, row7, row_low = row == 0, row == 7, row < 4
    lane0, lane127, col_low = lane == 0, lane == 127, col < 4

    edge_rows = (row_low & (me[1] == sizes[1] - 1)) | (~row_low & (me[1] == 0))
    edge_cols = (col_low & (me[2] == 0)) | (~col_low & (me[2] == sizes[2] - 1))
    keep_first, keep_last = (me[0] > 0).astype(F32), (me[0] < sizes[0] - 1).astype(F32)

    def mirror_rows(tiles, spill):
        image = jnp.where((row == 1) | (row == 4), rot(tiles, 2, tiles.ndim - 2), jnp.where(
            (row == 2) | (row == 5), rot(tiles, 4, tiles.ndim - 2),
            jnp.where((row == 3) | (row == 6), rot(tiles, 6, tiles.ndim - 2), 0.0)))
        return jnp.where(edge_rows, -image, spill)

    def mirror_cols(packed, spill):
        image = jnp.where(col == 0, rot(packed, -6, 1), jnp.where(col == 1, rot(packed, -4, 1), jnp.where(
            col == 2, rot(packed, -2, 1), jnp.where(col == 5, rot(packed, 2, 1), jnp.where(
                col == 6, rot(packed, 4, 1), jnp.where(col == 7, rot(packed, 6, 1), 0.0))))))
        return jnp.where(edge_cols, -image, spill)

    def part(n, ref, per, g):
        return ref.at[n, pl.ds(2 * per * g, per if isinstance(g, int) and g == 2 else 2 * per)]

    def gas_x(n):
        return ((-1, 1)[n], 0, 0), sx_v.at[n, pl.ds(20, 3)], rx_v.at[1 - n, pl.ds(20, 3)], x_ss.at[n], gx_rs.at[1 - n]

    def send_gas_x(to_origin):
        for n in range(2):
            send([gas_x(n)], to_origin)

    def send_y(g):
        for n in range(2):
            send([((0, (-1, 1)[n], 0), part(n, sy_v, 7, g), part(1 - n, ry_v, 7, g), y_ss.at[n], y_rs.at[1 - n, g])], False)

    def send_zd():
        for n, (a, b) in enumerate(DIAG):
            send([((0, a, b), sd_v.at[n, pl.ds(0, 5)], rd_v.at[3 - n, pl.ds(0, 5)], d_ss.at[n], d_rs.at[3 - n, 0])], False)
        for n in range(2):
            send([((0, 0, (-1, 1)[n]), sz_v.at[n, pl.ds(0, 10)], rz_v.at[1 - n, pl.ds(0, 10)], z_ss.at[n],
                   z_rs.at[1 - n, 0])], False)

    def wait_part(step, dst, rsem):
        _, ok, origin = near(step)

        @pl.when(ok if origin is None else ok & jnp.logical_not(origin))
        def _():
            copy(step, dst, dst, rsem, rsem).wait_recv()

    def wait_y(g):
        for n in range(2):
            @pl.when(jnp.logical_not(is_origin))
            def _():
                wait_recv((0, (-1, 1)[n], 0), part(n, ry_v, 7, g), y_rs.at[n, g])

    def wait_zd():
        @pl.when(jnp.logical_not(is_origin))
        def _():
            for n in range(2):
                wait_part((0, 0, (-1, 1)[n]), rz_v.at[n, pl.ds(0, 10)], z_rs.at[n, 0])
            for n, (a, b) in enumerate(DIAG):
                wait_part((0, a, b), rd_v.at[n, pl.ds(0, 5)], d_rs.at[n, 0])

    AROUND = ((2, sz_v, 1, bz_v), (1, sd_v, 3, bd_v))

    def send_around(g):
        first, last = ((0, 4), (4, 5))[g]
        for n, ((a, b), (per, src, at_n, dst)) in enumerate(zip(SIDES[1:], AROUND)):
            tiles = pl.ds(per * first, per * (last - first))
            for x in range(2):
                copy((x, a, b), src.at[at_n, tiles], dst.at[tiles], o_ss.at[n], b_rs.at[g]).start()
            if g:
                tiles = pl.ds(0, 5 * per)
                copy((2, a, b), src.at[at_n, tiles], dst.at[tiles], o_ss.at[n], b_rs.at[0]).start()

    def origin_y(g):
        return (0, 1, 0), part(1, sy_v, 7, g), part(0, ry_v, 7, g), y_ss.at[1], y_rs.at[0, g]

    def take_gas(n):
        wait_recv(((-1, 1)[n], 0, 0), rx_v.at[n, pl.ds(20, 3)], gx_rs.at[n])
        for j in range(3):
            gas_v[j, 5 * n] = rx_v[n, 20 + j]

    def pack(planes, first):
        result = jnp.zeros((8, 128), F32)
        for i in range(planes.shape[0]):
            result = jnp.where(slot == first + i, rot(planes[i], 8 * (first + i) + 4, 1), result)
        return result

    def spread_gas():
        for j in range(3):
            sgz_v[j] = pack(gas_v[j], 4)
            for i in range(6):
                sy_v[0, 35 + j, pl.ds(i, 1), :] = gas_v[j, i, pl.ds(0, 1), :]
                sy_v[1, 35 + j, pl.ds(i, 1), :] = gas_v[j, i, pl.ds(7, 1), :]
            for n in range(2):
                sy_v[n, 35 + j, pl.ds(6, 2), :] = jnp.zeros((2, 128), F32)
        for n in range(2):
            send([((0, (-1, 1)[n], 0), sy_v.at[n, pl.ds(35, 3)], ry_v.at[1 - n, pl.ds(35, 3)], y_ss.at[n], y_rs.at[1 - n, 3])])
            send([((0, 0, (-1, 1)[n]), sgz_v, rz_v.at[1 - n, pl.ds(10, 3)], z_ss.at[n], z_rs.at[1 - n, 1])])
        for n, (a, b) in enumerate(DIAG):
            send([((0, a, b), sgz_v, rd_v.at[3 - n, pl.ds(5, 3)], d_ss.at[n], d_rs.at[3 - n, 1])])

    loads[0].wait()
    loads[1].wait()

    def products(s, carry):
        occ = jnp.where(counts_v[...] > s, F32(1.0), F32(0.0))
        occ_v[s] = occ
        weights, norm = [], None
        for axis in range(3):
            t = jnp.exp((0.5 - offsets_v[axis, s]) * INV_S2)
            low, mid = t * t, CENTRE * t
            total = low + mid + 1.0
            norm = total if norm is None else norm * total
            weights.append((low, mid))
        scale = occ / norm
        wx = (weights[0][0] * scale, weights[0][1] * scale, scale)
        for a in range(3):
            for b in range(3):
                xy = wx[a] * weights[1][b] if b < 2 else wx[a]
                for c in range(3):
                    prod_v[9 * a + 3 * b + c, s] = xy * weights[2][c] if c < 2 else xy
        return carry

    lax.fori_loop(0, 4, products, 0, unroll=True)
    loads[2].wait()
    for j in range(3):
        sx_v[0, 20 + j] = gas_v[j, 1]
        sx_v[1, 20 + j] = gas_v[j, 4]

    @pl.when(is_origin)
    def _():
        send_gas_x(None)
        for a, b in SIDES:
            copy((1, a, b), sx_v.at[1, pl.ds(20, 3)], rg_v, pg_ss, pg_rs).start()
        spread_gas()

    for load in loads[3:]:
        load.wait()
    for j in range(3):
        src_v[2 + j] = src_v[1] * pv_v[j]

    def unpack(tile, first, count):
        return jnp.stack([rot(tile, -(8 * (first + i) + 4), 1) for i in range(count)])

    def deposit(k, carry):
        src = [src_v[k, s] for s in range(4)]
        by_z = []
        for c in range(3):
            by_y = []
            for b in range(3):
                by_x = []
                for a in range(3):
                    total = src[0] * prod_v[9 * a + 3 * b + c, 0]
                    for s in range(1, 4):
                        total = total + src[s] * prod_v[9 * a + 3 * b + c, s]
                    by_x.append(total)
                lo, mid, hi = by_x
                by_y.append(jnp.concatenate([
                    lo[0:1], lo[1:2] + mid[0:1], lo[2:4] + mid[1:3] + hi[0:2], mid[3:4] + hi[2:3], hi[3:4]], axis=0))
            up, down = rot(by_y[2], 1, 1), rot(by_y[0], -1, 1)
            by_z.append((by_y[1] + jnp.where(row0, 0.0, up) + jnp.where(row7, 0.0, down),
                         jnp.where(row0, up, jnp.where(row7, down, 0.0))))
        main, packs = [], []
        for kind in range(2):
            up, down = rot(by_z[2][kind], 1, 2), rot(by_z[0][kind], -1, 2)
            spill = jnp.where(lane0, up, jnp.where(lane127, down, 0.0))
            main.append(by_z[1][kind] + jnp.where(lane0, 0.0, up) + jnp.where(lane127, 0.0, down))
            packed = rot(spill[0], 36, 1) * keep_first
            for i in range(1, 5):
                packed = packed + rot(spill[i], 8 * i + 36, 1)
            packs.append(packed + rot(spill[5], 76, 1) * keep_last)
        m, y = [jnp.concatenate([v[0:1] * keep_first, v[1:5], v[5:6] * keep_last], axis=0) for v in main]
        z, yz = packs
        y, yz = mirror_rows(m, y), mirror_rows(z, yz)
        mp, yp = pack(m, 4), pack(y, 4)
        z, yz = mirror_cols(mp, z), mirror_cols(yp, yz)
        dm_v[k], dy_v[k], dz_v[k], dyz_v[k] = m, y, z, yz
        sy_v[0, pl.ds(7 * k, 6)] = jnp.where(row_low, m, y)
        sy_v[1, pl.ds(7 * k, 6)] = jnp.where(row_low, y, m)
        sy_v[0, 7 * k + 6] = jnp.where(row_low, z, yz)
        sy_v[1, 7 * k + 6] = jnp.where(row_low, yz, z)
        zm = (jnp.where(col_low, z, mp), jnp.where(col_low, mp, z))
        zy = (jnp.where(col_low, yz, yp), jnp.where(col_low, yp, yz))
        for n in range(2):
            sz_v[n, 2 * k], sz_v[n, 2 * k + 1] = zm[n], zy[n]
        for n, (a, b) in enumerate(DIAG):
            first, second = (zm, zy) if a < 0 else (zy, zm)
            sd_v[n, k] = jnp.where(row_low, first[(b + 1) // 2], second[(b + 1) // 2])
        return carry

    def deposit_two(g, carry):
        deposit(2 * g, carry)
        deposit(2 * g + 1, carry)

        @pl.when(is_origin)
        def _():
            copy(*origin_y(g)).start()

            @pl.when(g == 1)
            def _():
                send_around(0)

        return carry

    lax.fori_loop(0, 2, deposit_two, 0)
    deposit(4, 0)

    @pl.when(is_origin)
    def _():
        send_around(1)
        copy(*origin_y(2)).start()

    @pl.when(jnp.logical_not(is_origin))
    def _():
        pl.semaphore_wait(barrier, greeted)
        send_gas_x(False)
        send_zd()
        for g in range(3):
            send_y(g)

    to_proxy = [(at(0, a, b), copy((1, -a, -b), src, dst, ssem, b_rs.at[n]))
                for n, ((a, b), src, dst, ssem) in enumerate((
                    (SIDES[0], sy_v.at[0, pl.ds(0, 35)], by_v, y_ss.at[0]),
                    (SIDES[1], sz_v.at[0, pl.ds(0, 10)], bz_v, z_ss.at[0]),
                    (SIDES[2], sd_v.at[0, pl.ds(0, 5)], bd_v, d_ss.at[0])))]
    for here, item in to_proxy:
        pl.when(here)(item.start)

    @pl.when(is_proxy)
    def _():
        for a, b in SIDES:
            copy((-1, a, b), sx_v.at[0, pl.ds(20, 3)], rg_v, pg_ss, pg_rs).start()

    by_origin = jnp.bool_(False)
    for step in ALL:
        if max(step) <= 0:
            by_origin = by_origin | near(step)[2]

    @pl.when(by_origin & jnp.logical_not(is_proxy))
    def _():
        pl.semaphore_wait(late_sem, 1)

    @pl.when(jnp.logical_not(is_origin))
    def _():
        @pl.when(jnp.logical_not(is_proxy))
        def _():
            take_gas(0)

        take_gas(1)
        spread_gas()


    def convolve(m, y, z, yz):
        edge_m, edge_y = unpack(z, 4, 6), unpack(yz, 4, 6)
        parts = [None] * 5

        def add(sum_s, sum_c, value):
            for d in range(5 - sum_s - sum_c):
                term = value * F32(TAPS[d, sum_s, sum_c])
                parts[d] = term if parts[d] is None else parts[d] + term

        for c in range(5):
            rows = []
            for kind, (tiles, edge) in enumerate(((m, edge_m), (y, edge_y))):
                if c and not (kind and c == 4):
                    tiles = (rot(jnp.where(lane < c, edge, tiles), -c, 2)
                             + rot(jnp.where(lane >= 128 - c, edge, tiles), c, 2))
                rows.append(tiles)
            add(0, c, rows[0])
            for s in range(1, 5 - c):
                add(s, c, rot(jnp.where(row < s, rows[1], rows[0]), -s, 1)
                    + rot(jnp.where(row >= 8 - s, rows[1], rows[0]), s, 1))
        pushed = [None] * 14
        for i in range(6):
            for d in range(5):
                for q in {i + 4 - d, i + 4 + d}:
                    pushed[q] = parts[d][i] if pushed[q] is None else pushed[q] + parts[d][i]
        return pushed

    turn = is_proxy.astype(jnp.int32)
    row_in = row + turn * (7 - 2 * row) < 4
    col_in = col + turn * (7 - 2 * col) < 4
    first_x = (me[0] == 0).astype(F32)
    ends = (lane0 | lane127)[None]

    def around(k):
        tiles, halo, diag = by_v[pl.ds(7 * k, 6)], by_v[7 * k + 6], bd_v[k]
        low_m = bz_v[2 * k] + jnp.where(row_in, diag, 0.0)
        low_y = bz_v[2 * k + 1] + jnp.where(row_in, 0.0, diag)
        m = jnp.where(row_in[None], tiles, 0.0) + jnp.where(ends, unpack(jnp.where(col_in, 0.0, low_m), 4, 6), 0.0)
        y = jnp.where(row_in[None], 0.0, tiles) + jnp.where(ends, unpack(jnp.where(col_in, 0.0, low_y), 4, 6), 0.0)
        z = jnp.where(row_in, halo, 0.0) + jnp.where(col_in, low_m, 0.0)
        yz = jnp.where(row_in, 0.0, halo) + jnp.where(col_in, low_y, 0.0)
        pushed = convolve(m, y, z, yz)
        own = [pushed[5 + i] - pushed[3 - i] for i in range(3)] + [pushed[8]]
        return own, pushed[9:13], pushed[13]

    def filter_one(k, carry):
        below, above = ry_v[0, pl.ds(7 * k, 6)], ry_v[1, pl.ds(7 * k, 6)]
        below_z, above_z = ry_v[0, 7 * k + 6], ry_v[1, 7 * k + 6]
        m = dm_v[k] + jnp.where(row_low[None], below, above)
        y = dy_v[k] + jnp.where(row_low[None], above, below)
        side = []
        for n, b in enumerate((0, 1)):
            lower, upper = rd_v[b, k], rd_v[2 + b, k]
            side.append((rz_v[n, 2 * k] + jnp.where(row_low, lower, upper),
                         rz_v[n, 2 * k + 1] + jnp.where(row_low, upper, lower)))
        z = dz_v[k] + jnp.where(col_low, side[0][0], side[1][0]) + jnp.where(row_low, below_z, above_z)
        yz = dyz_v[k] + jnp.where(col_low, side[0][1], side[1][1]) + jnp.where(row_low, above_z, below_z)
        m = m + jnp.where(ends, unpack(jnp.where(col_low, side[1][0], side[0][0]), 4, 6), 0.0)
        y = y + jnp.where(ends, unpack(jnp.where(col_low, side[1][1], side[0][1]), 4, 6), 0.0)
        pushed = convolve(m, y, z, yz)
        for i in range(4):
            sx_v[0, 4 * k + i] = pushed[1 + i]
            filtered_o[k, i] = pushed[5 + i]
            sx_v[1, 4 * k + i] = pushed[9 + i]
        sx2_v[0, k] = pushed[0]
        sx2_v[1, k] = pushed[13]

        @pl.when(me[0] == 0)
        def _():
            for i in range(3):
                rx_v[0, 4 * k + i] = -pushed[3 - i]

        @pl.when(me[0] == sizes[0] - 1)
        def _():
            for i in range(1, 4):
                rx_v[1, 4 * k + i] = -pushed[13 - i]
        return carry

    def push(first, count, to_origin=None):
        for n, s in enumerate((-1, 1)):
            tiles = pl.ds(4 * first, 4 * count)
            send([((s, 0, 0), sx_v.at[n, tiles], rx_v.at[1 - n, tiles], x_ss.at[n], x_rs.at[1 - n])], to_origin)

    def push_far(to_origin=None):
        for n, s in enumerate((-1, 1)):
            send([((2 * s, 0, 0), sx2_v.at[n], rx2_v.at[1 - n], x2_ss.at[n], x2_rs.at[1 - n])], to_origin)

    def filter_and_push(k, carry):
        filter_one(k, carry)

        @pl.when(jnp.logical_not(is_proxy))
        def _():
            push(k, 1)

        return carry

    def filter_two(g, carry):
        wait_y(g)
        filter_and_push(2 * g, carry)
        filter_and_push(2 * g + 1, carry)
        return carry

    wait_zd()
    lax.fori_loop(0, 2, filter_two, 0)
    wait_y(2)
    filter_and_push(4, 0)

    @pl.when(jnp.logical_not(is_proxy))
    def _():
        push_far()

    def around_one(k, carry):
        for g in range(2):
            first, last = ((0, 4), (4, 5))[g]
            for a, (per, _, _, dst) in enumerate(AROUND):
                part_in = dst.at[pl.ds(per * first, per * (last - first))]

                @pl.when((k == first) & (is_late[0] | is_late[1]) & (me[1] == a))
                def _():
                    copy((0, 0, -1), part_in, part_in, b_rs.at[g], b_rs.at[g]).wait_recv()

        @pl.when((k == 0) & is_proxy)
        def _():
            for n, dst in enumerate((by_v, bz_v, bd_v)):
                copy((-1, 0, 0), dst, dst, b_rs.at[n], b_rs.at[n]).wait_recv()

        @pl.when(is_proxy | is_late[0] | is_late[1])
        def _():
            own, right, far = around(k)
            for i in range(4):
                filtered_o[k, i] += own[i] * first_x + right[i] * (1.0 - first_x)

            @pl.when(is_proxy)
            def _():
                for i in range(4):
                    sx_v[0, 4 * k + i] += own[i]
                sx_v[1, 4 * k] += far

        return carry

    lax.fori_loop(0, 5, around_one, 0)

    @pl.when(is_proxy)
    def _():
        push(0, 5, False)
        push_far(False)
        pl.semaphore_wait(late_sem, 1)
        send_gas_x(True)
        push(0, 5, True)
        push_far(True)

    @pl.when(is_origin)
    def _():
        take_gas(1)

    @pl.when(is_proxy)
    def _():
        take_gas(0)


    for n in range(2):
        wait_recv((0, (-1, 1)[n], 0), ry_v.at[n, pl.ds(35, 3)], y_rs.at[n, 3])
        wait_recv((0, 0, (-1, 1)[n]), rz_v.at[n, pl.ds(10, 3)], z_rs.at[n, 1])
    for n, (a, b) in enumerate(DIAG):
        wait_recv((0, a, b), rd_v.at[n, pl.ds(5, 3)], d_rs.at[n, 1])

    @pl.when(is_beside[0] | is_beside[1])
    def _():
        copy((1, 0, 0), rg_v, rg_v, pg_rs, pg_rs).wait_recv()

    for x, i in ((0, 5), (1, 0)):
        @pl.when(at(x, 1, 0))
        def _():
            for j in range(3):
                ry_v[0, 35 + j, pl.ds(i, 1), :] = rg_v[j, pl.ds(7, 1), :]

        for y, ref, tile in ((0, rz_v, 10), (1, rd_v, 5)):
            @pl.when(at(x, y, 1))
            def _():
                for j in range(3):
                    ref[0, tile + j] = jnp.where(slot == 4 + i, rot(rg_v[j], 8 * i + 36, 1), ref[0, tile + j])

    def shift(j, carry):
        tiles = gas_v[j]
        below, above = ry_v[0, 35 + j], ry_v[1, 35 + j]
        rows = jnp.stack([jnp.where(row0, jnp.broadcast_to(above[i:i + 1], (8, 128)),
                                    jnp.broadcast_to(below[i:i + 1], (8, 128))) for i in range(6)])
        halo_m = jnp.where(col_low, rz_v[0, 10 + j], rz_v[1, 10 + j])
        halo_y = jnp.where(col_low, jnp.where(row0, rd_v[2, 5 + j], rd_v[0, 5 + j]),
                           jnp.where(row0, rd_v[3, 5 + j], rd_v[1, 5 + j]))
        variants = []
        for value, halo in ((tiles, halo_m), (rows, halo_y)):
            edge = unpack(halo, 4, 6)
            variants.append((rot(jnp.where(lane127[None], edge, value), 1, 2), value,
                             rot(jnp.where(lane0[None], edge, value), -1, 2)))
        for c in range(3):
            value, halo = variants[0][c], variants[1][c]
            shifted_v[j, c] = rot(jnp.where(row7[None], halo, value), 1, 1)
            shifted_v[j, 3 + c] = value
            shifted_v[j, 6 + c] = rot(jnp.where(row0[None], halo, value), -1, 1)
        return carry

    lax.fori_loop(0, 3, shift, 0, unroll=True)

    def drag(x, carry):
        totals = [jnp.zeros((4, 8, 128), F32) for _ in range(3)]
        for a in range(3):
            for bc in range(9):
                weight = prod_v[9 * a + bc, :, x]
                for j in range(3):
                    totals[j] = totals[j] + weight * shifted_v[j, bc, x + a][None]
        for j in range(3):
            drag_o[j, :, x] = src_v[1, :, x] * totals[j] - occ_v[:, x] * src_v[2 + j, :, x]
        return carry

    lax.fori_loop(0, 4, drag, 0, unroll=True)

    @pl.when(is_late[2])
    def _():
        for a, dst in enumerate((bz_v, bd_v)):
            @pl.when(me[1] == a)
            def _():
                copy((0, 0, -1), dst, dst, b_rs.at[0], b_rs.at[0]).wait_recv()

        for k in range(5):
            low_m = bz_v[2 * k] + jnp.where(row_in, bd_v[k], 0.0)
            spill = jnp.where(lane0 | lane127, rot(jnp.where(col_in, 0.0, low_m), -76, 1), 0.0)
            filtered_o[k, 0] += spill * F32(TAPS[4, 0, 0])

    for n, s in enumerate((-1, 1)):
        wait_recv((s, 0, 0), rx_v.at[n, pl.ds(0, 20)], x_rs.at[n])
        wait_recv((2 * s, 0, 0), rx2_v.at[n], x2_rs.at[n])
    for k in range(5):
        for i in range(4):
            total = filtered_o[k, i] + (rx_v[0, 4 * k + i] + rx_v[1, 4 * k + i])
            if i in (0, 3):
                total = total + rx2_v[i // 3, k]
            filtered_o[k, i] = total

    for n, s in enumerate((-1, 1)):
        wait_send((s, 0, 0), sx_v.at[n], x_ss.at[n])
        wait_send((2 * s, 0, 0), sx2_v.at[n], x2_ss.at[n])

    @pl.when(jnp.logical_not(is_origin))
    def _():
        for n, s in enumerate((-1, 1)):
            wait_send((0, s, 0), sy_v.at[n], y_ss.at[n])
            wait_send((0, 0, s), sz_v.at[n], z_ss.at[n])
        for n, (a, b) in enumerate(DIAG):
            wait_send((0, a, b), sd_v.at[n], d_ss.at[n])

    @pl.when(is_origin)
    def _():
        wait_send((0, 1, 0), sy_v.at[1], y_ss.at[1])
        for ssem in (z_ss.at[1], d_ss.at[3]):
            copy((1, 0, 0), sgz_v, sgz_v, ssem, ssem).wait_send()
        for n, ref in enumerate((sy_v.at[0, pl.ds(0, 30)], sx_v.at[0, pl.ds(0, 15)])):
            copy((1, 0, 0), ref, ref, o_ss.at[n], o_ss.at[n]).wait_send()

    @pl.when(is_origin | is_proxy)
    def _():
        nine = sx_v.at[0, pl.ds(0, 9)]
        copy((1, 0, 0), nine, nine, pg_ss, pg_ss).wait_send()


def store(filtered_v, drag_v, filtered_h, drag_h, sem):
    copies = [pltpu.make_async_copy(filtered_v, filtered_h, sem.at[0]), pltpu.make_async_copy(drag_v, drag_h, sem.at[1])]
    for item in copies:
        item.start()
    for item in copies:
        item.wait()


def solution(mesh):
    sizes = tuple(mesh.shape[name] for name in ("gx", "gy", "gz"))
    dma = pltpu.SemaphoreType.DMA

    def vmem(*shape):
        return pltpu.VMEM(shape + (8, 128), F32)

    def shards(counts, offsets, volume, beta, particle_velocity, gas_velocity):
        any_space = pl.BlockSpec(memory_space=pl.ANY)
        out_shape = (jax.ShapeDtypeStruct((5, 4, 8, 128), F32), jax.ShapeDtypeStruct((3, 4, 4, 8, 128), F32))
        filtered, drag = pl.pallas_call(
            functools.partial(kernel, sizes),
            out_shape=out_shape,
            in_specs=[any_space] * 6,
            out_specs=(pl.BlockSpec(memory_space=pltpu.VMEM),) * 2,
            scratch_shapes=[
                pltpu.VMEM((4, 8, 128), jnp.int32), vmem(3, 4, 4), vmem(5, 4, 4), vmem(3, 4, 4), vmem(3, 6),
                vmem(4, 4), vmem(27, 4, 4), vmem(3, 9, 6), vmem(5, 6), vmem(5, 6), vmem(5), vmem(5),
                vmem(2, 38), vmem(2, 13), vmem(4, 8), vmem(2, 23), vmem(2, 5),
                vmem(2, 38), vmem(2, 13), vmem(4, 8), vmem(2, 23), vmem(2, 5), vmem(3),
                vmem(35), vmem(10), vmem(5), vmem(3),
                dma((6,)), dma((2,)), dma((2,)), dma((4,)), dma((2,)), dma((2,)),
                dma((2, 4)), dma((2, 2)), dma((4, 2)), dma((2,)), dma((2,)), dma((2,)), pltpu.SemaphoreType.REGULAR,
                dma((3,)), dma((2,)), dma, dma,
            ],
            compiler_params=pltpu.CompilerParams(
                collective_id=0, has_side_effects=True, vmem_limit_bytes=32 * 2**20),
            name="deposit_filter_drag",
        )(*[pltpu.with_memory_space_constraint(v, pltpu.HBM) for v in (
            counts, offsets, volume, beta, particle_velocity, gas_velocity)])
        return pl.pallas_call(
            store, out_shape=out_shape, in_specs=[any_space] * 2, out_specs=(any_space,) * 2,
            scratch_shapes=[dma((2,))], compiler_params=pltpu.CompilerParams(vmem_limit_bytes=2**20), name="store",
        )(filtered, drag)

    in_specs = (
        P("gx", "gy", "gz"),
        P(None, None, "gx", "gy", "gz"),
        P(None, "gx", "gy", "gz"),
        P(None, "gx", "gy", "gz"),
        P(None, None, "gx", "gy", "gz"),
        P(None, "gx", "gy", "gz"),
    )
    out_specs = (P(None, "gx", "gy", "gz"), P(None, None, "gx", "gy", "gz"))
    return jax.shard_map(shards, mesh=mesh, in_specs=in_specs, out_specs=out_specs, check_vma=False)
```
